32 devices in a mesh: gx: 8 (over z, y), gy: 4 (over x, core).
Axes of the slice: x: 2, y: 2, z: 4, core: 2. Of those that a mesh axis runs over, the one named last changes fastest.
Arguments:
- right_side: float32 [3, 64, 64, 512], P(None, None, 'gx', 'gy'), may hold values from -8 to 8
- material: int32 [64, 64, 512], P(None, 'gx', 'gy'), may hold values from 0 to 15
- conductivity: float32 [16], replicated, may hold values from 0.1 to 10
Outputs:
- corrected: float32 [3, 64, 64, 512], P(None, None, 'gx', 'gy')
- final_residual: float32 [3, 64, 64, 512], P(None, None, 'gx', 'gy')
The draws below stay inside these ranges and needn't reach their ends.
Inputs may be any that keep to these rules, and one draw needn't show every extreme that they name: material class of each cell, an index into conductivity.
All inputs are finite; a program needn't handle non-finite values.
Results may differ from the reference program's by a relative error of at most 0.00002.
Values sent between devices are 32-bit elements; how exact they have to be, the bound alone decides.
No kernel may reach another device: no remote copies, remote signals or barrier semaphores. Data moves between devices by JAX's collectives and lax.ppermute only.
A program may use at most 64 MiB of HBM per device.

```python
import math
import jax
import jax.numpy as jnp
from jax import lax

NZ = 64
NCLASS = 16
NX = 64
NY = 512


def plant(drawn, key, smallest, top_value):
    place = [jax.random.randint(jax.random.fold_in(key, axis), (), 0, length) for axis, length in enumerate(drawn.shape)]
    main_axis = drawn.shape.index(max(drawn.shape))
    beside = place[:main_axis] + [(place[main_axis] + 1) % drawn.shape[main_axis]] + place[main_axis + 1:]
    return drawn.at[tuple(place)].set(smallest).at[tuple(beside)].set(top_value)


def steps_of(stream_key, dims, shards, least, largest):
    loudness, own = 1.0, jax.random.fold_in(stream_key, 6)
    for dim, parts in shards:
        heights = jnp.exp(jax.random.uniform(jax.random.fold_in(own, dim), (parts,), jnp.float32, least / len(shards), largest / len(shards)))
        loudness = loudness * jnp.repeat(heights, dims[dim] // parts).reshape([-1 if axis == dim else 1 for axis in range(len(dims))])
    return loudness


def bell_draw(key, extent, scale, bound, cuts=(), dtype=jnp.bfloat16):
    level = steps_of(key, extent, cuts, -0.22, 0.18) if cuts else 1.0
    values = jax.random.normal(key, extent, jnp.float32) * scale * level
    return jnp.minimum(jnp.maximum(values, -bound), bound).astype(dtype)


def setup_inputs(seed: int = 0) -> dict:
    key_of = jax.random.split(jax.random.key(seed), 4)
    right_side = bell_draw(key_of[0], (3, NZ, NX, NY), 1.0, 8.0, ((2, 8), (3, 4)), jnp.float32)
    material = plant(jax.random.randint(key_of[1], (NZ, NX, NY), 0, NCLASS), jax.random.fold_in(key_of[1], 1), 0, NCLASS - 1).astype(jnp.int32)
    conductivity = jnp.clip(jnp.exp(jax.random.uniform(key_of[2], (NCLASS,), jnp.float32, math.log(0.1), math.log(10.0))), 0.1, 10.0)
    return dict(right_side=right_side, material=material, conductivity=conductivity)


OMEGA_EDGE = 0.6
OMEGA_NODE = 0.7
OMEGA_VECTOR = 0.5
across_z = 0
across_x = 1
across_y = 2


def forward(values, dimension):
    count = values.shape[dimension]
    widths = [(0, 0)] * values.ndim
    widths[dimension] = (0, 1)
    return lax.slice_in_dim(jnp.pad(values, widths), 1, count + 1, axis=dimension)


def backward(values, dimension):
    count = values.shape[dimension]
    widths = [(0, 0)] * values.ndim
    widths[dimension] = (1, 0)
    return lax.slice_in_dim(jnp.pad(values, widths), 0, count, axis=dimension)


def curl_faces(edge_x, edge_y, edge_z):
    face_z = edge_x - forward(edge_x, across_y) + forward(edge_y, across_x) - edge_y
    face_x = edge_y - forward(edge_y, across_z) + forward(edge_z, across_y) - edge_z
    face_y = edge_z - forward(edge_z, across_x) + forward(edge_x, across_z) - edge_x
    return face_x, face_y, face_z


def curl_edges(face_x, face_y, face_z):
    edge_x = face_z - backward(face_z, across_y) - face_y + backward(face_y, across_z)
    edge_y = backward(face_z, across_x) - face_z + face_x - backward(face_x, across_z)
    edge_z = backward(face_x, across_y) - face_x + face_y - backward(face_y, across_x)
    return jnp.stack([edge_x, edge_y, edge_z])


def operator(field, sigma_cell):
    face_x, face_y, face_z = curl_faces(field[0], field[1], field[2])
    return curl_edges(face_x, face_y, face_z) + sigma_cell[None] * field


def node_operator(potential, sigma_cell):
    total = jnp.zeros_like(potential)
    for dimension in (across_x, across_y, across_z):
        flux_part = sigma_cell * (forward(potential, dimension) - potential)
        total = total + backward(flux_part, dimension) - flux_part
    return total


def reference(right_side, material, conductivity):
    sigma_cell = conductivity[material]
    diagonal = 4.0 + sigma_cell
    first = OMEGA_EDGE * right_side / diagonal[None]
    residual = right_side - operator(first, sigma_cell)
    directions = (across_x, across_y, across_z)
    node_rhs = jnp.zeros_like(sigma_cell)
    for component in range(3):
        part = residual[component]
        node_rhs = node_rhs + backward(part, directions[component]) - part
    node_diag = 3.0 * sigma_cell + backward(sigma_cell, across_x) + backward(sigma_cell, across_y) + backward(sigma_cell, across_z)
    phi_first = OMEGA_NODE * node_rhs / node_diag
    phi_second = phi_first + OMEGA_NODE * (node_rhs - node_operator(phi_first, sigma_cell)) / node_diag
    pieces = []
    for component in range(3):
        dimension = directions[component]
        part = residual[component]
        projected = (part + backward(part, dimension)) / 2.0
        scale = (diagonal + backward(diagonal, dimension)) / 4.0
        psi_part = OMEGA_VECTOR * projected / scale
        pieces.append(forward(phi_second, dimension) - phi_second + (psi_part + forward(psi_part, dimension)) / 2.0)
    corrected = first + jnp.stack(pieces)
    final_residual = right_side - operator(corrected, sigma_cell)
    return corrected, final_residual
```

```python
import functools

import jax
import jax.numpy as jnp
from jax import lax
from jax.experimental import pallas as pl
from jax.experimental.pallas import tpu as pltpu
from jax.sharding import PartitionSpec as P

OMEGA_EDGE = 0.6
OMEGA_NODE = 0.7
F32 = jnp.float32
LANES = 128
TILE = 8
REACH = 2
WIDE = 2 * REACH
COLS = 2 * WIDE
PAD = 8


def lanes():
    return lax.broadcasted_iota(jnp.int32, (TILE, LANES), 1)


def class_table(conductivity):
    lane = lanes()
    table = jnp.zeros((TILE, LANES), F32)
    for category in range(conductivity.shape[0]):
        table = jnp.where(lane == category, conductivity[category], table)
    return table


def pick(table, index):
    return jnp.take_along_axis(table, index, axis=1)


def turn(value, amount):
    amount = amount % LANES
    return value if amount == 0 else pltpu.roll(value, amount, 1)


def gather_edges(place, conductivity, source, material, edges, rows_a, rows_b):
    cells_x = source.shape[1] // edges.shape[0]
    depth = edges.shape[0]
    lane = lanes()
    table = class_table(conductivity)
    even = place[0] % 2 == 0
    row_a = jnp.where(even, cells_x - REACH, 0)
    row_b = jnp.where(even, 0, cells_x - REACH)

    def tile(step, carry):
        base = pl.multiple_of(step * TILE, TILE)

        def load(field, row):
            where = pl.ds(base * cells_x + row, TILE, stride=cells_x)
            if field < 3:
                return source[field, where, :]
            return pick(table, material[where, :])

        packed = jnp.zeros((TILE, LANES), F32)
        for field in range(4):
            for row in range(cells_x):
                slot = (field * cells_x + row) * WIDE
                value = turn(load(field, row), slot + REACH)
                packed = jnp.where((lane >= slot) & (lane < slot + WIDE), value, packed)
        edges[pl.ds(base, TILE), :] = packed
        for out, first in ((rows_a, row_a), (rows_b, row_b)):
            for row in range(REACH):
                for field in range(4):
                    out[row * 4 + field, pl.ds(base, TILE), :] = load(field, first + row)
        return carry

    lax.fori_loop(0, depth // TILE, tile, 0, unroll=2)


def strip_index(cells_x, field, row, column):
    return (field * cells_x + row) * WIDE + column % WIDE


def strip_source(column, own, left, right):
    return jnp.where(column < REACH, left, jnp.where(column < COLS - REACH, own, right))


def corner_strips(place, own, got_a, got_b, cells_x, out):
    depth = own.shape[0]
    lane = lanes()
    per_field = LANES // 4
    field, rank, column = lane // per_field, (lane % per_field) // COLS, lane % COLS
    row = jnp.where(rank < REACH, rank, cells_x - 2 * REACH + rank)
    index = strip_index(cells_x, field, row, column)
    even = place[1] % 2 == 0

    def tile(step, carry):
        where = pl.ds(pl.multiple_of(step * TILE, TILE), TILE)
        mine, a, b = (pick(ref[where, :], index) for ref in (own, got_a, got_b))
        left, right = jnp.where(even, b, a), jnp.where(even, a, b)
        out[where, :] = strip_source(column, mine, left, right)
        return carry

    lax.fori_loop(0, depth // TILE, tile, 0, unroll=True)


def pack_corners(cells_x, place, own, got_a, got_b, rows_a, rows_b, out_a, out_b):
    count = rows_a.shape[0]
    corner_strips(place, own, got_a, got_b, cells_x, out_a.at[count])
    out_b[count] = out_a[count]
    out_a[:count] = rows_a[...]
    out_b[:count] = rows_b[...]


FIRST = ("sx", "fx", "fy", "fz")
FACES = ("face_x", "face_y", "face_z", "q_y", "coef")
RESIDUALS = ("res_x", "res_y", "res_z", "node", "phi")
NODES = ("flow_y", "phi2", "psi_x", "psi_y", "psi_z")
LAST = ("mid_x", "mid_y", "mid_z", "turn_x", "turn_y", "turn_z")
NAMES = FIRST + FACES + RESIDUALS + NODES + LAST


def cycle(
    cells_x,
    sizes,
    place,
    conductivity,
    source,
    material,
    own,
    got_a,
    got_b,
    rows_a,
    rows_b,
    corrected,
    final,
    *scratch,
):
    ref = dict(zip(NAMES, scratch))
    depth = own.shape[0]
    tiles = depth // TILE
    rows = cells_x + 2 * REACH
    strip = rows
    lane = lanes()
    level = lax.broadcasted_iota(jnp.int32, (TILE, LANES), 0)
    table = class_table(conductivity)
    even_x = place[0] % 2 == 0
    even_y = place[1] % 2 == 0
    has_low = jnp.where(place[0] > 0, 1.0, 0.0).astype(F32)
    has_high = jnp.where(place[0] < sizes[0] - 1, 1.0, 0.0).astype(F32)
    first_col = jnp.where(place[1] > 0, 1.0, 0.0).astype(F32)

    zeros = jnp.zeros((PAD, LANES), F32)
    for name in NAMES:
        for i in range(rows + 1):
            ref[name][i, pl.ds(0, PAD), :] = zeros
            ref[name][i, pl.ds(PAD + depth, PAD), :] = zeros

    strip_row = lane // COLS - REACH
    column = lane % COLS
    strip_col = jnp.where(column < WIDE, column - REACH, column - WIDE - REACH + LANES)

    def inside(index, axis, length):
        total = sizes[axis] * length
        at = index + place[axis] * length
        return (at >= 0) & (at < total)

    used = lane < rows * COLS
    in_x, in_y = inside(strip_row, 0, cells_x), inside(strip_col, 1, LANES)
    strip_mask = jnp.where(in_x & in_y & used, 1.0, 0.0).astype(F32)
    strip_back_x = jnp.where(inside(strip_row - 1, 0, cells_x), 4.0, 0.0).astype(F32)
    strip_back_y = jnp.where(inside(strip_col - 1, 1, LANES), 4.0, 0.0).astype(F32)
    main_back_y = jnp.where(lane == 0, 4.0 * first_col, 4.0).astype(F32)

    def mask(i):
        if i == strip:
            return strip_mask
        if i < REACH:
            return has_low
        if i >= rows - REACH:
            return has_high
        return None

    def masked(value, i):
        m = mask(i)
        return value if m is None else value * m

    def over(top, bottom, i):
        m = mask(i)
        return top / bottom if m is None else (top * m) / (bottom + (1.0 - m))

    def sweep(body):
        def step(t, carry):
            body(pl.multiple_of(t * TILE, TILE))
            return carry

        lax.fori_loop(0, tiles, step, 0, unroll=2)

    class At:
        def __init__(self, base):
            self.base = pl.multiple_of(base + PAD, TILE)

        def __call__(self, name, i, dz=0):
            return ref[name][i, pl.ds(self.base + dz, TILE), :]

        def put(self, name, i, value):
            ref[name][i, pl.ds(self.base, TILE), :] = value

        def fz(self, name, i):
            return self(name, i, 1)

        def bz(self, name, i):
            return self(name, i, -1)

        def fx(self, name, i):
            return turn(self(name, i), -COLS) if i == strip else self(name, i + 1)

        def bx(self, name, i):
            return turn(self(name, i), COLS) if i == strip else self(name, i - 1)

        def fy(self, name, i):
            moved = turn(self(name, i), -1)
            if i == strip:
                return moved
            edge = turn(self(name, strip), LANES - 1 - (i * COLS + COLS - REACH))
            return jnp.where(lane == LANES - 1, edge, moved)

        def by(self, name, i):
            moved = turn(self(name, i), 1)
            if i == strip:
                return moved
            edge = turn(self(name, strip), -(i * COLS + REACH - 1))
            return jnp.where(lane == 0, edge, moved)

    def span(low, high):
        return list(range(low + REACH, high + REACH + 1)) + [strip]

    own_index = [strip_index(cells_x, f, jnp.clip(strip_row, 0, cells_x - 1), column) for f in range(4)]

    def start(base):
        at = At(base)
        where = pl.ds(base, TILE)

        def fill(i, values):
            sigma = values[3]
            weight = OMEGA_EDGE / (4.0 + sigma)
            at.put("sx", i, sigma)
            for name, value in zip(("fx", "fy", "fz"), values):
                at.put(name, i, value * weight)

        for row in range(cells_x):
            pick_rows = pl.ds(base * cells_x + row, TILE, stride=cells_x)
            fill(
                row + REACH,
                [source[f, pick_rows, :] for f in range(3)] + [pick(table, material[pick_rows, :])],
            )
        for row in range(REACH):
            a = [rows_a[row * 4 + f, where, :] for f in range(4)]
            b = [rows_b[row * 4 + f, where, :] for f in range(4)]
            fill(row, [jnp.where(even_x, v, u) for u, v in zip(a, b)])
            fill(row + rows - REACH, [jnp.where(even_x, u, v) for u, v in zip(a, b)])
        corner_a, corner_b = rows_a[4 * REACH, where, :], rows_b[4 * REACH, where, :]
        low = jnp.where(even_x, corner_b, corner_a)
        high = jnp.where(even_x, corner_a, corner_b)
        mine, a, b = own[where, :], got_a[where, :], got_b[where, :]
        left, right = jnp.where(even_y, b, a), jnp.where(even_y, a, b)
        values = []
        per_field = LANES // 4
        for f in range(4):
            v = strip_source(
                column, pick(mine, own_index[f]), pick(left, own_index[f]), pick(right, own_index[f])
            )
            v = jnp.where(lane < REACH * COLS, turn(low, -(f * per_field + REACH * COLS)), v)
            far = (rows - REACH) * COLS
            v = jnp.where(lane >= far, turn(high, far - f * per_field), v)
            values.append(jnp.where(used, v, 0.0))
        fill(strip, values)

    sweep(start)

    def faces(base):
        at = At(base)
        for i in span(-2, 8):
            x, y, z = at("fx", i), at("fy", i), at("fz", i)
            at.put("face_z", i, masked(x - at.fy("fx", i) + at.fx("fy", i) - y, i))
            at.put("face_y", i, masked(z - at.fx("fz", i) + at.fz("fx", i) - x, i))
            at.put("face_x", i, masked(y - at.fz("fy", i) + at.fy("fz", i) - z, i))
        for i in span(-1, 9):
            sigma = at("sx", i)
            diag = 3.0 * sigma + at.bx("sx", i) + at.by("sx", i) + at.bz("sx", i)
            at.put("coef", i, over(OMEGA_NODE, diag, i))
            at.put("q_y", i, at("fy", i) * (sigma * (2.0 / 3.0) + 20.0 / 3.0))

    sweep(faces)

    def scale(sigma):
        return sigma * (2.0 / 3.0) + 20.0 / 3.0

    def residuals(base):
        at = At(base)
        for i in span(-2, 8):
            g = scale(at("sx", i))
            face_y, face_z = at("face_y", i), at("face_z", i)
            edge = face_z - at.by("face_z", i) - face_y + at.bz("face_y", i)
            at.put("res_x", i, at("fx", i) * g - edge)
            if i == 0:
                continue
            face_x = at("face_x", i)
            edge = at.bx("face_z", i) - face_z + face_x - at.bz("face_x", i)
            at.put("res_y", i, at("q_y", i) - edge)
            edge = at.by("face_x", i) - face_x + face_y - at.bx("face_y", i)
            at.put("res_z", i, at("fz", i) * g - edge)
        for i in span(-1, 9):
            g = scale(at("sx", i))
            q_x, q_z = at("fx", i) * g, at("fz", i) * g
            if i == strip:
                back_x = turn(q_x, COLS)
            else:
                back_x = at("fx", i - 1) * scale(at("sx", i - 1))
            back_z = at.bz("fz", i) * scale(at.bz("sx", i))
            rhs = back_x - q_x + at.by("q_y", i) - at("q_y", i) + back_z - q_z
            at.put("node", i, rhs)
            at.put("phi", i, at("coef", i) * rhs)

    sweep(residuals)

    def potentials(base):
        at = At(base)
        for i in span(-1, 8):
            at.put("flow_y", i, at("sx", i) * (at.fy("phi", i) - at("phi", i)))

    sweep(potentials)

    def second(base):
        at = At(base)
        for i in span(0, 8):
            sigma, phi = at("sx", i), at("phi", i)
            flow_x = sigma * (at.fx("phi", i) - phi)
            back_x = at.bx("sx", i) * (phi - at.bx("phi", i))
            flow_z = sigma * (at.fz("phi", i) - phi)
            back_z = at.bz("sx", i) * (phi - at.bz("phi", i))
            applied = back_x - flow_x + at.by("flow_y", i) - at("flow_y", i) + back_z - flow_z
            at.put("phi2", i, phi + at("coef", i) * (at("node", i) - applied))
        back_z_const = jnp.where((level == 0) & (base == 0), 4.0, 8.0).astype(F32)
        for i in span(-1, 8):
            sigma = at("sx", i)
            if i == strip:
                const_x, const_y = strip_back_x + 4.0, strip_back_y + 4.0
            else:
                const_y = main_back_y + 4.0
                const_x = 8.0
                if i - REACH in (-1, 0):
                    const_x = 4.0 + 4.0 * has_low
            for d, const, back in (
                ("x", const_x, at.bx),
                ("y", const_y, at.by),
                ("z", back_z_const, at.bz),
            ):
                total = sigma + back("sx", i) + const
                at.put("psi_" + d, i, over(at("res_" + d, i) + back("res_" + d, i), total, i))

    sweep(second)

    def middles(base):
        at = At(base)
        for i in span(-1, 8):
            if i != rows - REACH:
                at.put("mid_x", i, 0.5 * (at("psi_x", i) + at.fx("psi_x", i)))
            at.put("mid_y", i, 0.5 * (at("psi_y", i) + at.fy("psi_y", i)))
            at.put("mid_z", i, 0.5 * (at("psi_z", i) + at.fz("psi_z", i)))

    sweep(middles)

    def turns(base):
        at = At(base)
        for i in span(-1, 7):
            x, y, z = at("mid_x", i), at("mid_y", i), at("mid_z", i)
            at.put("turn_z", i, masked(x - at.fy("mid_x", i) + at.fx("mid_y", i) - y, i))
            at.put("turn_y", i, masked(z - at.fx("mid_z", i) + at.fz("mid_x", i) - x, i))
            at.put("turn_x", i, masked(y - at.fz("mid_y", i) + at.fy("mid_z", i) - z, i))

    sweep(turns)

    def finish(base):
        at = At(base)
        for row in range(cells_x):
            i = row + REACH
            where = pl.ds(base * cells_x + row, TILE, stride=cells_x)
            sigma, phi = at("sx", i), at("phi2", i)
            x, y, z = at("turn_x", i), at("turn_y", i), at("turn_z", i)
            edges = (
                z - at.by("turn_z", i) - y + at.bz("turn_y", i),
                at.bx("turn_z", i) - z + x - at.bz("turn_x", i),
                at.by("turn_x", i) - x + y - at.bx("turn_y", i),
            )
            for f, (d, ahead) in enumerate((("x", at.fx), ("y", at.fy), ("z", at.fz))):
                change = ahead("phi2", i) - phi + at("mid_" + d, i)
                corrected[f, where, :] = at("f" + d, i) + change
                final[f, where, :] = at("res_" + d, i) - edges[f] - sigma * change

    sweep(finish)


def swaps(count, first):
    pairs = [(i, i + 1) for i in range(first, count - 1, 2)]
    return pairs + [(j, i) for i, j in pairs]


def local(right_side, material, conductivity):
    depth, cells_x, cells_y = material.shape
    size_x, size_y = lax.axis_size("gx"), lax.axis_size("gy")
    place = jnp.stack([lax.axis_index("gx"), lax.axis_index("gy")]).astype(jnp.int32)
    source = right_side.reshape(3, depth * cells_x, cells_y)
    classes = material.reshape(depth * cells_x, cells_y)
    vmem = pl.BlockSpec(memory_space=pltpu.VMEM)
    smem = pl.BlockSpec(memory_space=pltpu.SMEM)
    slab = jax.ShapeDtypeStruct((depth, cells_y), F32)
    params = pltpu.CompilerParams(vmem_limit_bytes=48 * 2**20)

    own, rows_a, rows_b = pl.pallas_call(
        gather_edges,
        out_shape=(
            slab,
            jax.ShapeDtypeStruct((4 * REACH, depth, cells_y), F32),
            jax.ShapeDtypeStruct((4 * REACH, depth, cells_y), F32),
        ),
        in_specs=[smem, smem, vmem, vmem],
        out_specs=(vmem, vmem, vmem),
        compiler_params=params,
        name="gather_edges",
    )(place, conductivity, source, classes)
    got_b = lax.ppermute(own, "gy", swaps(size_y, 1))
    got_a = lax.ppermute(own, "gy", swaps(size_y, 0))
    wide = jax.ShapeDtypeStruct((4 * REACH + 1, depth, cells_y), F32)
    send_a, send_b = pl.pallas_call(
        functools.partial(pack_corners, cells_x),
        out_shape=(wide, wide),
        in_specs=[smem] + [vmem] * 5,
        out_specs=(vmem, vmem),
        compiler_params=params,
        name="pack_corners",
    )(place, own, got_a, got_b, rows_a, rows_b)
    rows_b = lax.ppermute(send_b, "gx", swaps(size_x, 1))
    rows_a = lax.ppermute(send_a, "gx", swaps(size_x, 0))
    held = pltpu.VMEM((cells_x + 2 * REACH + 1, depth + 2 * PAD, cells_y), F32)
    flat = jax.ShapeDtypeStruct((3, depth * cells_x, cells_y), F32)
    corrected, final = pl.pallas_call(
        functools.partial(cycle, cells_x, (size_x, size_y)),
        out_shape=(flat, flat),
        in_specs=[smem, smem] + [vmem] * 7,
        out_specs=(vmem, vmem),
        scratch_shapes=[held] * len(NAMES),
        compiler_params=params,
        name="cycle",
    )(place, conductivity, source, classes, own, got_a, got_b, rows_a, rows_b)
    return corrected.reshape(right_side.shape), final.reshape(right_side.shape)


def solution(mesh):
    return jax.shard_map(
        local,
        mesh=mesh,
        in_specs=(P(None, None, "gx", "gy"), P(None, "gx", "gy"), P()),
        out_specs=(P(None, None, "gx", "gy"), P(None, None, "gx", "gy")),
        check_vma=False,
    )
```

```python
import functools

import jax
import jax.numpy as jnp
from jax import lax
from jax.experimental import pallas as pl
from jax.experimental.pallas import tpu as pltpu
from jax.sharding import PartitionSpec as P

OMEGA_EDGE = 0.6
OMEGA_NODE = 0.7
F32 = jnp.float32
LANES = 128
TILE = 8
REACH = 2
WIDE = 2 * REACH
COLS = 2 * WIDE
EARLY_FLOPS = 10**10
PAD = 8


def lanes():
    return lax.broadcasted_iota(jnp.int32, (TILE, LANES), 1)


def class_table(conductivity):
    lane = lanes()
    table = jnp.zeros((TILE, LANES), F32)
    for category in range(conductivity.shape[0]):
        table = jnp.where(lane == category + 1, conductivity[category], table)
    return table


def pick(table, index):
    return jnp.take_along_axis(table, index, axis=1)


def turn(value, amount):
    amount = amount % LANES
    return value if amount == 0 else pltpu.roll(value, amount, 1)


def code(material):
    return (material + 1).astype(F32)


def gather_edges(cells_x, place, source, material, edges, rows_a, rows_b):
    depth = edges.shape[0]
    lane = lanes()
    even = place[0] % 2 == 0
    row_a = jnp.where(even, cells_x - REACH, 0)
    row_b = jnp.where(even, 0, cells_x - REACH)

    for base in range(0, depth, TILE):

        def load(field, row):
            where = pl.ds(base * cells_x + row, TILE, stride=cells_x)
            return source[field, where, :] if field < 3 else code(material[where, :])

        packed = jnp.zeros((TILE, LANES), F32)
        for field in range(4):
            for row in range(cells_x):
                slot = (field * cells_x + row) * WIDE
                value = turn(load(field, row), slot + REACH)
                packed = jnp.where((lane >= slot) & (lane < slot + WIDE), value, packed)
        edges[pl.ds(base, TILE), :] = packed
        for out, first in ((rows_a, row_a), (rows_b, row_b)):
            for row in range(REACH):
                for field in range(4):
                    out[row * 4 + field, pl.ds(base, TILE), :] = load(field, first + row)


def strip_index(cells_x, field, row, column):
    return (field * cells_x + row) * WIDE + column % WIDE


def strip_source(column, own, left, right):
    return jnp.where(column < REACH, left, jnp.where(column < COLS - REACH, own, right))


def corner_strips(cells_x, place, own, got_a, got_b, rows_b, out, all_b):
    depth = own.shape[0]
    lane = lanes()
    per_field = LANES // 4
    field, rank, column = lane // per_field, (lane % per_field) // COLS, lane % COLS
    row = jnp.where(rank < REACH, rank, cells_x - 2 * REACH + rank)
    index = strip_index(cells_x, field, row, column)
    even = place[1] % 2 == 0
    for base in range(0, depth, TILE):
        where = pl.ds(base, TILE)
        mine, a, b = (pick(ref[where, :], index) for ref in (own, got_a, got_b))
        left, right = jnp.where(even, b, a), jnp.where(even, a, b)
        value = strip_source(column, mine, left, right)
        out[where, :] = value
        all_b[4 * REACH, where, :] = value


READS = {
    "sx": (),
    "fx": (),
    "fy": (),
    "fz": (),
    "face_x": (("fy", 0), ("fz", 0)),
    "face_y": (("fz", 0), ("fz", 1), ("fx", 0)),
    "face_z": (("fx", 0), ("fy", 0), ("fy", 1)),
    "coef": (("sx", 0), ("sx", -1)),
    "q_y": (("fy", 0), ("sx", 0)),
    "res_x": (("fx", 0), ("sx", 0), ("face_z", 0), ("face_y", 0)),
    "res_y": (("q_y", 0), ("face_z", -1), ("face_z", 0), ("face_x", 0)),
    "res_z": (("fz", 0), ("sx", 0), ("face_x", 0), ("face_y", 0), ("face_y", -1)),
    "node": (("fx", 0), ("sx", 0), ("fx", -1), ("sx", -1), ("q_y", 0), ("fz", 0)),
    "phi": (("coef", 0), ("node", 0)),
    "flow_y": (("sx", 0), ("phi", 0)),
    "psi_x": (("res_x", 0), ("res_x", -1), ("sx", 0), ("sx", -1)),
    "psi_y": (("res_y", 0), ("sx", 0)),
    "psi_z": (("res_z", 0), ("sx", 0)),
    "phi2": (
        ("sx", 0),
        ("sx", -1),
        ("phi", 0),
        ("phi", 1),
        ("phi", -1),
        ("flow_y", 0),
        ("coef", 0),
        ("node", 0),
    ),
    "mid_x": (("psi_x", 0), ("psi_x", 1)),
    "mid_y": (("psi_y", 0),),
    "mid_z": (("psi_z", 0),),
    "turn_x": (("mid_y", 0), ("mid_z", 0)),
    "turn_y": (("mid_z", 0), ("mid_z", 1), ("mid_x", 0)),
    "turn_z": (("mid_x", 0), ("mid_y", 0), ("mid_y", 1)),
    "out": (
        ("turn_x", 0),
        ("turn_y", 0),
        ("turn_y", -1),
        ("turn_z", 0),
        ("turn_z", -1),
        ("phi2", 0),
        ("phi2", 1),
        ("mid_x", 0),
        ("mid_y", 0),
        ("mid_z", 0),
        ("fx", 0),
        ("fy", 0),
        ("fz", 0),
        ("sx", 0),
        ("res_x", 0),
        ("res_y", 0),
        ("res_z", 0),
    ),
}
NAMES = tuple(name for name in READS if name != "out")
Z_READ = ("sx", "fx", "fy", "fz", "face_x", "face_y", "res_z", "phi")
Z_READ += ("phi2", "psi_z", "mid_x", "mid_y", "turn_x", "turn_y")
PASSES = (
    ("sx", "fx", "fy", "fz"),
    ("face_x", "face_y", "face_z", "coef", "q_y"),
    ("res_x", "res_y", "res_z", "node", "phi"),
    ("flow_y", "psi_x", "psi_y", "psi_z"),
    ("phi2", "mid_x", "mid_y", "mid_z"),
    ("turn_x", "turn_y", "turn_z"),
    ("out",),
)


class Plan:
    def __init__(self, cells_x, low_is_late):
        self.cells_x = cells_x
        need = {("out", row) for row in range(cells_x)}
        todo = list(need)
        while todo:
            name, row = todo.pop()
            for read, offset in READS[name]:
                if (read, row + offset) not in need:
                    need.add((read, row + offset))
                    todo.append((read, row + offset))

        def early(name, row):
            if not READS[name]:
                return row >= 0 if low_is_late else row < cells_x
            return all(early(read, row + offset) for read, offset in READS[name])

        order = {name: rank for rank, name in enumerate(READS)}
        need = sorted(need, key=lambda item: (order[item[0]], item[1]))
        self.early = [item for item in need if early(*item)]
        self.late = [item for item in need if not early(*item)]
        used = {(read, row + offset) for name, row in self.late for read, offset in READS[name]}
        self.kept = [item for item in self.early if item in used]


def run_cycle(plan, late, low_is_late, sizes, place, table, fetch, strips, slots, strip_ref, emit, depth):
    cells_x = plan.cells_x
    rows = cells_x + 2 * REACH
    lane = lanes()
    level = lax.broadcasted_iota(jnp.int32, (TILE, LANES), 0)
    has_low = jnp.where(place[0] > 0, 1.0, 0.0).astype(F32)
    has_high = jnp.where(place[0] < sizes[0] - 1, 1.0, 0.0).astype(F32)
    first_col = jnp.where(place[1] > 0, 4.0, 0.0).astype(F32)
    todo = plan.late if late else plan.early
    strip = None

    zeros = jnp.zeros((PAD, LANES), F32)
    for name, row in todo:
        if name in Z_READ:
            ref, slot = slots[name, row]
            ref[slot, pl.ds(0, PAD), :] = zeros
            ref[slot, pl.ds(PAD + depth, PAD), :] = zeros
    for name in Z_READ:
        strip_ref[NAMES.index(name), pl.ds(0, PAD), :] = zeros
        strip_ref[NAMES.index(name), pl.ds(PAD + depth, PAD), :] = zeros

    strip_row = lane // COLS - REACH
    column = lane % COLS
    strip_col = jnp.where(column < WIDE, column - REACH, column - WIDE - REACH + LANES)

    def inside(index, axis, length):
        at = index + place[axis] * length
        return (at >= 0) & (at < sizes[axis] * length)

    held = lane < rows * COLS
    if not late:
        held &= strip_row >= 0 if low_is_late else strip_row < cells_x
    in_x, in_y = inside(strip_row, 0, cells_x), inside(strip_col, 1, LANES)
    strip_mask = jnp.where(in_x & in_y & held, 1.0, 0.0).astype(F32)
    strip_back_x = jnp.where(inside(strip_row - 1, 0, cells_x), 8.0, 4.0).astype(F32)
    strip_back_y = jnp.where(inside(strip_col - 1, 1, LANES), 8.0, 4.0).astype(F32)
    main_back_y = 4.0 + jnp.where(lane == 0, first_col, 4.0).astype(F32)

    def mask(row):
        if row is strip:
            return strip_mask
        if row < 0:
            return has_low
        return has_high if row >= cells_x else None

    def masked(value, row):
        m = mask(row)
        return value if m is None else value * m

    def over(top, bottom, row):
        m = mask(row)
        return top / bottom if m is None else (top * m) / (bottom + (1.0 - m))

    def scale(sigma):
        return sigma * (2.0 / 3.0) + 20.0 / 3.0

    class At:
        def __init__(self, base):
            self.base = base
            self.seen = {}

        def where(self, name, row, dz=0):
            ref, slot = (strip_ref, NAMES.index(name)) if row is strip else slots[name, row]
            return ref, slot, pl.ds(self.base + PAD + dz, TILE)

        def __call__(self, name, row, dz=0):
            key = (name, row, dz)
            if key not in self.seen:
                ref, slot, rows_z = self.where(name, row, dz)
                self.seen[key] = ref[slot, rows_z, :]
            return self.seen[key]

        def put(self, name, row, value):
            ref, slot, rows_z = self.where(name, row)
            ref[slot, rows_z, :] = value
            self.seen[name, row, 0] = value

        def fz(self, name, row):
            return self(name, row, 1)

        def bz(self, name, row):
            return self(name, row, -1)

        def fx(self, name, row):
            return turn(self(name, row), -COLS) if row is strip else self(name, row + 1)

        def bx(self, name, row):
            return turn(self(name, row), COLS) if row is strip else self(name, row - 1)

        def fy(self, name, row):
            moved = turn(self(name, row), -1)
            if row is strip:
                return moved
            start = (row + REACH) * COLS + COLS - REACH
            edge = turn(self(name, strip), LANES - 1 - start)
            return jnp.where(lane == LANES - 1, edge, moved)

        def by(self, name, row):
            moved = turn(self(name, row), 1)
            if row is strip:
                return moved
            edge = turn(self(name, strip), -((row + REACH) * COLS + REACH - 1))
            return jnp.where(lane == 0, edge, moved)

    def first_pass(at, row, names):
        x, y, z, codes = strips(at.base) if row is strip else fetch(at.base, row)
        sigma = pick(table, codes.astype(jnp.int32))
        weight = OMEGA_EDGE / (4.0 + sigma)
        for name, value in (("sx", sigma), ("fx", x * weight), ("fy", y * weight), ("fz", z * weight)):
            if name in names:
                at.put(name, row, value)

    def face_pass(at, row, names):
        if "face_x" in names:
            value = at("fy", row) - at.fz("fy", row) + at.fy("fz", row) - at("fz", row)
            at.put("face_x", row, masked(value, row))
        if "face_y" in names:
            value = at("fz", row) - at.fx("fz", row) + at.fz("fx", row) - at("fx", row)
            at.put("face_y", row, masked(value, row))
        if "face_z" in names:
            value = at("fx", row) - at.fy("fx", row) + at.fx("fy", row) - at("fy", row)
            at.put("face_z", row, masked(value, row))
        if "coef" in names:
            diag = 3.0 * at("sx", row) + at.bx("sx", row) + at.by("sx", row) + at.bz("sx", row)
            at.put("coef", row, over(OMEGA_NODE, diag, row))
        if "q_y" in names:
            at.put("q_y", row, at("fy", row) * scale(at("sx", row)))

    def residual_pass(at, row, names):
        g = scale(at("sx", row))
        if "res_x" in names:
            z, y = at("face_z", row), at("face_y", row)
            edge = z - at.by("face_z", row) - y + at.bz("face_y", row)
            at.put("res_x", row, at("fx", row) * g - edge)
        if "res_y" in names:
            z, x = at("face_z", row), at("face_x", row)
            edge = at.bx("face_z", row) - z + x - at.bz("face_x", row)
            at.put("res_y", row, at("q_y", row) - edge)
        if "res_z" in names:
            x, y = at("face_x", row), at("face_y", row)
            edge = at.by("face_x", row) - x + y - at.bx("face_y", row)
            at.put("res_z", row, at("fz", row) * g - edge)
        if "node" in names:
            q_x = at("fx", row) * g
            if row is strip:
                back_x = turn(q_x, COLS)
            else:
                back_x = at("fx", row - 1) * scale(at("sx", row - 1))
            back_z = at.bz("fz", row) * scale(at.bz("sx", row))
            change_y = at.by("q_y", row) - at("q_y", row)
            at.put("node", row, back_x - q_x + change_y + back_z - at("fz", row) * g)
        if "phi" in names:
            at.put("phi", row, at("coef", row) * at("node", row))

    def flow_pass(at, row, names):
        if "flow_y" in names:
            at.put("flow_y", row, at("sx", row) * (at.fy("phi", row) - at("phi", row)))
        if row is strip:
            const_x, const_y = strip_back_x, strip_back_y
        else:
            const_y = main_back_y
            const_x = 4.0 + 4.0 * has_low if row in (-1, 0) else 8.0
        const_z = jnp.where(level == 0, 4.0, 8.0).astype(F32) if at.base == 0 else 8.0
        for name, const, back in (("x", const_x, at.bx), ("y", const_y, at.by), ("z", const_z, at.bz)):
            if "psi_" + name in names:
                total = at("sx", row) + back("sx", row) + const
                value = at("res_" + name, row) + back("res_" + name, row)
                at.put("psi_" + name, row, over(value, total, row))

    def middle_pass(at, row, names):
        if "phi2" in names:
            sigma, phi = at("sx", row), at("phi", row)
            flow_x = sigma * (at.fx("phi", row) - phi)
            back_x = at.bx("sx", row) * (phi - at.bx("phi", row))
            flow_z = sigma * (at.fz("phi", row) - phi)
            back_z = at.bz("sx", row) * (phi - at.bz("phi", row))
            change_y = at.by("flow_y", row) - at("flow_y", row)
            applied = back_x - flow_x + change_y + back_z - flow_z
            at.put("phi2", row, phi + at("coef", row) * (at("node", row) - applied))
        for name, ahead in (("x", at.fx), ("y", at.fy), ("z", at.fz)):
            if "mid_" + name in names:
                at.put("mid_" + name, row, 0.5 * (at("psi_" + name, row) + ahead("psi_" + name, row)))

    def turn_pass(at, row, names):
        if "turn_x" in names:
            value = at("mid_y", row) - at.fz("mid_y", row) + at.fy("mid_z", row) - at("mid_z", row)
            at.put("turn_x", row, masked(value, row))
        if "turn_y" in names:
            value = at("mid_z", row) - at.fx("mid_z", row) + at.fz("mid_x", row) - at("mid_x", row)
            at.put("turn_y", row, masked(value, row))
        if "turn_z" in names:
            value = at("mid_x", row) - at.fy("mid_x", row) + at.fx("mid_y", row) - at("mid_y", row)
            at.put("turn_z", row, masked(value, row))

    def last_pass(at, row, names):
        sigma, phi = at("sx", row), at("phi2", row)
        x, y, z = at("turn_x", row), at("turn_y", row), at("turn_z", row)
        edges = (
            z - at.by("turn_z", row) - y + at.bz("turn_y", row),
            at.bx("turn_z", row) - z + x - at.bz("turn_x", row),
            at.by("turn_x", row) - x + y - at.bx("turn_y", row),
        )
        for f, (name, ahead) in enumerate((("x", at.fx), ("y", at.fy), ("z", at.fz))):
            change = ahead("phi2", row) - phi + at("mid_" + name, row)
            final = at("res_" + name, row) - edges[f] - sigma * change
            emit(at.base, row, f, at("f" + name, row) + change, final)

    steps = (first_pass, face_pass, residual_pass, flow_pass, middle_pass, turn_pass, last_pass)
    for names, step in zip(PASSES, steps):
        wanted = [item for item in todo if item[0] in names]
        for base in range(0, depth, TILE):
            at = At(base)
            if step is not last_pass:
                step(at, strip, names)
            for row in sorted({row for _, row in wanted}):
                step(at, row, [name for name in names if (name, row) in wanted])


def strip_reader(cells_x, place, own, got_a, got_b, corner_low, corner_high):
    lane = lanes()
    rows = cells_x + 2 * REACH
    row = jnp.clip(lane // COLS - REACH, 0, cells_x - 1)
    column = lane % COLS
    index = [strip_index(cells_x, f, row, column) for f in range(4)]
    even = place[1] % 2 == 0
    per_field = LANES // 4
    far = (rows - REACH) * COLS

    def strips(base):
        where = pl.ds(base, TILE)
        mine, a, b = own[where, :], got_a[where, :], got_b[where, :]
        left, right = jnp.where(even, b, a), jnp.where(even, a, b)
        values = []
        for f in range(4):
            v = strip_source(column, pick(mine, index[f]), pick(left, index[f]), pick(right, index[f]))
            v = jnp.where((lane < REACH * COLS) | (lane >= far), 0.0, v)
            if corner_low is not None:
                moved = turn(corner_low[where, :], -(f * per_field + REACH * COLS))
                v = jnp.where(lane < REACH * COLS, moved, v)
            if corner_high is not None:
                moved = turn(corner_high[where, :], far - f * per_field)
                v = jnp.where((lane >= far) & (lane < rows * COLS), moved, v)
            values.append(v)
        return values

    return strips


def early_rows(
    plans,
    sizes,
    place,
    conductivity,
    source,
    material,
    own,
    got_a,
    got_b,
    rows_a,
    corner_a,
    kept,
    corrected,
    final,
    scratch,
    strip_ref,
):
    depth = own.shape[0]
    table = class_table(conductivity)
    for parity, plan in enumerate(plans):

        @pl.when(place[0] % 2 == parity)
        def _(plan=plan, low_is_late=parity == 0):
            cells_x = plan.cells_x

            def fetch(base, row):
                if 0 <= row < cells_x:
                    where = pl.ds(base * cells_x + row, TILE, stride=cells_x)
                    return [source[f, where, :] for f in range(3)] + [code(material[where, :])]
                first = (row - cells_x if low_is_late else row + REACH) * 4
                return [rows_a[first + f, pl.ds(base, TILE), :] for f in range(4)]

            def emit(base, row, f, value, rest):
                where = pl.ds(base * cells_x + row, TILE, stride=cells_x)
                corrected[f, where, :] = value
                final[f, where, :] = rest

            corners = (None, corner_a) if low_is_late else (corner_a, None)
            strips = strip_reader(cells_x, place, own, got_a, got_b, *corners)
            slots = {item: (kept, i) for i, item in enumerate(plan.kept)}
            others = [item for item in plan.early if item not in slots and item[0] != "out"]
            slots |= {item: (scratch, i) for i, item in enumerate(others)}
            run_cycle(
                plan, False, low_is_late, sizes, place, table, fetch, strips, slots, strip_ref, emit, depth
            )


def late_rows(
    plans,
    sizes,
    place,
    conductivity,
    own,
    got_a,
    got_b,
    corner_a,
    rows_b,
    kept,
    part_corrected,
    part_final,
    corrected,
    final,
    scratch,
    strip_ref,
):
    depth = own.shape[0]
    table = class_table(conductivity)
    for f in range(3):
        corrected[f] = part_corrected[f]
        final[f] = part_final[f]
    for parity, plan in enumerate(plans):

        @pl.when(place[0] % 2 == parity)
        def _(plan=plan, low_is_late=parity == 0):
            cells_x = plan.cells_x
            corner_b = rows_b.at[4 * REACH]

            def fetch(base, row):
                first = (row + REACH if low_is_late else row - cells_x) * 4
                return [rows_b[first + f, pl.ds(base, TILE), :] for f in range(4)]

            def emit(base, row, f, value, rest):
                where = pl.ds(base * cells_x + row, TILE, stride=cells_x)
                corrected[f, where, :] = value
                final[f, where, :] = rest

            corners = (corner_b, corner_a) if low_is_late else (corner_a, corner_b)
            strips = strip_reader(cells_x, place, own, got_a, got_b, *corners)
            slots = {item: (kept, i) for i, item in enumerate(plan.kept)}
            others = [item for item in plan.late if item[0] != "out"]
            slots |= {item: (scratch, i) for i, item in enumerate(others)}
            run_cycle(
                plan, True, low_is_late, sizes, place, table, fetch, strips, slots, strip_ref, emit, depth
            )


def swaps(count, first):
    pairs = [(i, i + 1) for i in range(first, count - 1, 2)]
    return pairs + [(j, i) for i, j in pairs]


def local(right_side, material, conductivity):
    depth, cells_x, cells_y = material.shape
    size_x, size_y = lax.axis_size("gx"), lax.axis_size("gy")
    place = jnp.stack([lax.axis_index("gx"), lax.axis_index("gy")]).astype(jnp.int32)
    source = right_side.reshape(3, depth * cells_x, cells_y)
    classes = material.reshape(depth * cells_x, cells_y)
    vmem = pl.BlockSpec(memory_space=pltpu.VMEM)
    smem = pl.BlockSpec(memory_space=pltpu.SMEM)
    slab = jax.ShapeDtypeStruct((depth, cells_y), F32)

    def slabs(count):
        return jax.ShapeDtypeStruct((count, depth, cells_y), F32)

    def padded(count):
        return (count, depth + 2 * PAD, cells_y)

    def params(mib):
        return pltpu.CompilerParams(vmem_limit_bytes=mib * 2**20)

    own, rows_a, rows_b = pl.pallas_call(
        functools.partial(gather_edges, cells_x),
        out_shape=(slab, slabs(4 * REACH), slabs(4 * REACH + 1)),
        in_specs=[smem, vmem, vmem],
        out_specs=(vmem, vmem, vmem),
        compiler_params=params(16),
        name="gather_edges",
    )(place, source, classes)
    got_b = lax.ppermute(own, "gy", swaps(size_y, 1))
    got_a = lax.ppermute(own, "gy", swaps(size_y, 0))
    corners, rows_b = pl.pallas_call(
        functools.partial(corner_strips, cells_x),
        out_shape=(slab, slabs(4 * REACH + 1)),
        in_specs=[smem] + [vmem] * 4,
        out_specs=(vmem, vmem),
        input_output_aliases={4: 1},
        compiler_params=params(16),
        name="corner_strips",
    )(place, own, got_a, got_b, rows_b)
    corner_a = lax.ppermute(corners, "gx", swaps(size_x, 0))
    rows_b = lax.ppermute(rows_b, "gx", swaps(size_x, 1))
    rows_a = lax.ppermute(rows_a, "gx", swaps(size_x, 0))

    plans = [Plan(cells_x, low_is_late) for low_is_late in (True, False)]
    most_kept = max(len(plan.kept) for plan in plans)
    most_early = max(len(plan.early) for plan in plans)
    most_late = max(len(plan.late) for plan in plans)
    sizes = (size_x, size_y)
    flat = jax.ShapeDtypeStruct(source.shape, F32)
    strip_shape = pltpu.VMEM(padded(len(NAMES)), F32)
    kept, corrected, final = pl.pallas_call(
        functools.partial(early_rows, plans, sizes),
        out_shape=(jax.ShapeDtypeStruct(padded(most_kept), F32), flat, flat),
        in_specs=[smem, smem] + [vmem] * 7,
        out_specs=(vmem, vmem, vmem),
        scratch_shapes=[pltpu.VMEM(padded(most_early), F32), strip_shape],
        compiler_params=params(32),
        cost_estimate=pl.CostEstimate(flops=EARLY_FLOPS, bytes_accessed=0, transcendentals=0),
        name="early_rows",
    )(place, conductivity, source, classes, own, got_a, got_b, rows_a, corner_a)
    corrected, final = pl.pallas_call(
        functools.partial(late_rows, plans, sizes),
        out_shape=(flat, flat),
        in_specs=[smem, smem] + [vmem] * 8,
        out_specs=(vmem, vmem),
        scratch_shapes=[pltpu.VMEM(padded(most_late), F32), strip_shape],
        compiler_params=params(32),
        name="late_rows",
    )(place, conductivity, own, got_a, got_b, corner_a, rows_b, kept, corrected, final)
    return corrected.reshape(right_side.shape), final.reshape(right_side.shape)


def solution(mesh):
    return jax.shard_map(
        local,
        mesh=mesh,
        in_specs=(P(None, None, "gx", "gy"), P(None, "gx", "gy"), P()),
        out_specs=(P(None, None, "gx", "gy"), P(None, None, "gx", "gy")),
        check_vma=False,
    )
```

```python
import functools

import jax
import jax.numpy as jnp
from jax import lax
from jax.experimental import pallas as pl
from jax.experimental.pallas import tpu as pltpu
from jax.sharding import PartitionSpec as P

OMEGA_EDGE = 0.6
OMEGA_NODE = 0.7
F32 = jnp.float32
LANES = 128
TILE = 8
REACH = 2
WIDE = 2 * REACH
COLS = 2 * WIDE
EARLY_FLOPS = 10**9
RUNS = 4
PAD = 8


def lanes():
    return lax.broadcasted_iota(jnp.int32, (TILE, LANES), 1)


def class_table(conductivity):
    row = jnp.pad(conductivity, (1, LANES - 1 - conductivity.shape[0]))
    return jnp.broadcast_to(row[None], (TILE, LANES))


def pick(table, index):
    return jnp.take_along_axis(table, index, axis=1)


def turn(value, amount):
    amount = amount % LANES
    return value if amount == 0 else pltpu.roll(value, amount, 1)


def code(material):
    return (material + 1).astype(F32)


def gather(cells_x, place, fields, load, merge, edges, rows_a, rows_b, held):
    depth = edges.shape[0]
    lane = lanes()
    even = place[0] % 2 == 0
    row_a = jnp.where(even, cells_x - REACH, 0)
    row_b = jnp.where(even, 0, cells_x - REACH)
    for base in range(0, depth, TILE):
        where = pl.ds(base, TILE)
        packed = edges[where, :] if merge else jnp.zeros((TILE, LANES), F32)
        for field in fields:
            for row in range(cells_x):
                slot = (field * cells_x + row) * WIDE
                value = load(field, base, row)
                held[field, row, where, :] = value
                value = turn(value, slot + REACH)
                packed = jnp.where((lane >= slot) & (lane < slot + WIDE), value, packed)
            for out, first in ((rows_a, row_a), (rows_b, row_b)):
                for row in range(REACH):
                    out[row * 4 + field, where, :] = load(field, base, first + row)
        edges[where, :] = packed


def gather_classes(cells_x, place, material, edges, *outs):
    def load(field, base, row):
        return code(material[pl.ds(base * cells_x + row, TILE, stride=cells_x), :])

    gather(cells_x, place, (3,), load, False, edges, *outs)


def gather_source(cells_x, place, source, _edges, _rows_a, _rows_b, _held, edges, *outs):
    def load(field, base, row):
        return source[field, pl.ds(base * cells_x + row, TILE, stride=cells_x), :]

    gather(cells_x, place, range(3), load, True, edges, *outs)


def strip_index(cells_x, field, row, column):
    return (field * cells_x + row) * WIDE + column % WIDE


def strip_source(column, own, left, right):
    return jnp.where(column < REACH, left, jnp.where(column < COLS - REACH, own, right))


def corner_strips(cells_x, place, own, got_a, got_b, out):
    depth = own.shape[0]
    lane = lanes()
    per_field = LANES // 4
    field, rank, column = lane // per_field, (lane % per_field) // COLS, lane % COLS
    row = jnp.where(rank < REACH, rank, cells_x - 2 * REACH + rank)
    index = strip_index(cells_x, field, row, column)
    even = place[1] % 2 == 0
    for base in range(0, depth, TILE):
        where = pl.ds(base, TILE)
        mine, a, b = (pick(ref[where, :], index) for ref in (own, got_a, got_b))
        left, right = jnp.where(even, b, a), jnp.where(even, a, b)
        out[where, :] = strip_source(column, mine, left, right)


(SX, FX, FY, FZ, FACE_X, FACE_Y, FACE_Z, COEF, Q_Y) = range(9)
(RES_X, RES_Y, RES_Z, NODE, PHI, FLOW_Y, PSI_X, PSI_Y, PSI_Z) = range(9, 18)
(PHI2, MID_X, MID_Y, MID_Z, TURN_X, TURN_Y, TURN_Z, OUT) = range(18, 26)
COUNT = OUT

READS = {
    SX: (),
    FX: (),
    FY: (),
    FZ: (),
    FACE_X: ((FY, 0), (FZ, 0)),
    FACE_Y: ((FZ, 0), (FZ, 1), (FX, 0)),
    FACE_Z: ((FX, 0), (FY, 0), (FY, 1)),
    COEF: ((SX, 0), (SX, -1)),
    Q_Y: ((FY, 0), (SX, 0)),
    RES_X: ((FX, 0), (SX, 0), (FACE_Z, 0), (FACE_Y, 0)),
    RES_Y: ((Q_Y, 0), (FACE_Z, -1), (FACE_Z, 0), (FACE_X, 0)),
    RES_Z: ((FZ, 0), (SX, 0), (FACE_X, 0), (FACE_Y, 0), (FACE_Y, -1)),
    NODE: ((FX, 0), (SX, 0), (FX, -1), (SX, -1), (Q_Y, 0), (FZ, 0)),
    PHI: ((COEF, 0), (NODE, 0)),
    FLOW_Y: ((SX, 0), (PHI, 0)),
    PSI_X: ((RES_X, 0), (RES_X, -1), (SX, 0), (SX, -1)),
    PSI_Y: ((RES_Y, 0), (SX, 0)),
    PSI_Z: ((RES_Z, 0), (SX, 0)),
    PHI2: (
        (SX, 0),
        (SX, -1),
        (PHI, 0),
        (PHI, 1),
        (PHI, -1),
        (FLOW_Y, 0),
        (COEF, 0),
        (NODE, 0),
    ),
    MID_X: ((PSI_X, 0), (PSI_X, 1)),
    MID_Y: ((PSI_Y, 0),),
    MID_Z: ((PSI_Z, 0),),
    TURN_X: ((MID_Y, 0), (MID_Z, 0)),
    TURN_Y: ((MID_Z, 0), (MID_Z, 1), (MID_X, 0)),
    TURN_Z: ((MID_X, 0), (MID_Y, 0), (MID_Y, 1)),
    OUT: (
        (TURN_X, 0),
        (TURN_Y, 0),
        (TURN_Y, -1),
        (TURN_Z, 0),
        (TURN_Z, -1),
        (PHI2, 0),
        (PHI2, 1),
        (MID_X, 0),
        (MID_Y, 0),
        (MID_Z, 0),
        (FX, 0),
        (FY, 0),
        (FZ, 0),
        (SX, 0),
        (RES_X, 0),
        (RES_Y, 0),
        (RES_Z, 0),
    ),
}
Z_READ = (SX, FX, FY, FZ, FACE_X, FACE_Y, RES_Z, PHI)
Z_READ += (PHI2, PSI_Z, MID_X, MID_Y, TURN_X, TURN_Y)
PASSES = (
    (SX, FX, FY, FZ),
    (FACE_X, FACE_Y, FACE_Z, COEF, Q_Y),
    (RES_X, RES_Y, RES_Z, NODE, PHI),
    (FLOW_Y, PSI_X, PSI_Y, PSI_Z),
    (PHI2, MID_X, MID_Y, MID_Z),
    (TURN_X, TURN_Y, TURN_Z),
    (OUT,),
)


class Plan:
    def __init__(self, cells_x):
        self.cells_x = cells_x
        need = {(OUT, row) for row in range(cells_x)}
        todo = list(need)
        while todo:
            name, row = todo.pop()
            for read, offset in READS[name]:
                if (read, row + offset) not in need:
                    need.add((read, row + offset))
                    todo.append((read, row + offset))

        def early(name, row):
            if not READS[name]:
                return 0 <= row < cells_x
            return all(early(read, row + offset) for read, offset in READS[name])

        need = sorted(need)
        self.early = [item for item in need if early(*item)]
        self.late = [item for item in need if not early(*item)]
        used = {(read, row + offset) for name, row in self.late for read, offset in READS[name]}
        self.kept = [item for item in self.early if item in used]


def run_cycle(plan, late, sizes, place, table, fetch, strips, slots, strip_ref, emit, depth, leave=None):
    cells_x = plan.cells_x
    rows = cells_x + 2 * REACH
    lane = lanes()
    level = lax.broadcasted_iota(jnp.int32, (TILE, LANES), 0)
    has_low = jnp.where(place[0] > 0, 1.0, 0.0).astype(F32)
    has_high = jnp.where(place[0] < sizes[0] - 1, 1.0, 0.0).astype(F32)
    first_col = jnp.where(place[1] > 0, 4.0, 0.0).astype(F32)
    todo = plan.late if late else plan.early
    strip = None

    zeros = jnp.zeros((PAD, LANES), F32)
    for name, row in todo:
        if name in Z_READ:
            ref, slot = slots[name, row]
            ref[slot, pl.ds(0, PAD), :] = zeros
            ref[slot, pl.ds(PAD + depth, PAD), :] = zeros
    for name in Z_READ:
        strip_ref[name, pl.ds(0, PAD), :] = zeros
        strip_ref[name, pl.ds(PAD + depth, PAD), :] = zeros

    strip_row = lane // COLS - REACH
    column = lane % COLS
    strip_col = jnp.where(column < WIDE, column - REACH, column - WIDE - REACH + LANES)

    def inside(index, axis, length):
        at = index + place[axis] * length
        return (at >= 0) & (at < sizes[axis] * length)

    held = lane < rows * COLS
    if not late:
        held &= (strip_row >= 0) & (strip_row < cells_x)
    in_x, in_y = inside(strip_row, 0, cells_x), inside(strip_col, 1, LANES)
    strip_mask = jnp.where(in_x & in_y & held, 1.0, 0.0).astype(F32)
    strip_back_x = jnp.where(inside(strip_row - 1, 0, cells_x), 8.0, 4.0).astype(F32)
    strip_back_y = jnp.where(inside(strip_col - 1, 1, LANES), 8.0, 4.0).astype(F32)
    main_back_y = 4.0 + jnp.where(lane == 0, first_col, 4.0).astype(F32)

    def mask(row):
        if row is strip:
            return strip_mask
        if row < 0:
            return has_low
        return has_high if row >= cells_x else None

    def masked(value, row):
        m = mask(row)
        return value if m is None else value * m

    def over(top, bottom, row):
        m = mask(row)
        return top / bottom if m is None else (top * m) / (bottom + (1.0 - m))

    def scale(sigma):
        return sigma * (2.0 / 3.0) + 20.0 / 3.0

    class At:
        def __init__(self, base):
            self.base = base
            self.seen = {}

        def where(self, name, row, dz=0):
            ref, slot = (strip_ref, name) if row is strip else slots[name, row]
            return ref, slot, pl.ds(self.base + PAD + dz, TILE)

        def __call__(self, name, row, dz=0):
            key = (name, row, dz)
            if key not in self.seen:
                ref, slot, rows_z = self.where(name, row, dz)
                self.seen[key] = ref[slot, rows_z, :]
            return self.seen[key]

        def put(self, name, row, value):
            ref, slot, rows_z = self.where(name, row)
            ref[slot, rows_z, :] = value
            self.seen[name, row, 0] = value

        def fz(self, name, row):
            return self(name, row, 1)

        def bz(self, name, row):
            return self(name, row, -1)

        def fx(self, name, row):
            return turn(self(name, row), -COLS) if row is strip else self(name, row + 1)

        def bx(self, name, row):
            return turn(self(name, row), COLS) if row is strip else self(name, row - 1)

        def fy(self, name, row):
            moved = turn(self(name, row), -1)
            if row is strip:
                return moved
            start = (row + REACH) * COLS + COLS - REACH
            edge = turn(self(name, strip), LANES - 1 - start)
            return jnp.where(lane == LANES - 1, edge, moved)

        def by(self, name, row):
            moved = turn(self(name, row), 1)
            if row is strip:
                return moved
            edge = turn(self(name, strip), -((row + REACH) * COLS + REACH - 1))
            return jnp.where(lane == 0, edge, moved)

    def first_pass(at, row, names):
        x, y, z, codes = strips(at.base) if row is strip else fetch(at.base, row)
        sigma = pick(table, codes.astype(jnp.int32))
        weight = OMEGA_EDGE / (4.0 + sigma)
        for name, value in ((SX, sigma), (FX, x * weight), (FY, y * weight), (FZ, z * weight)):
            if name in names:
                at.put(name, row, value)

    def face_pass(at, row, names):
        if FACE_X in names:
            value = at(FY, row) - at.fz(FY, row) + at.fy(FZ, row) - at(FZ, row)
            at.put(FACE_X, row, masked(value, row))
        if FACE_Y in names:
            value = at(FZ, row) - at.fx(FZ, row) + at.fz(FX, row) - at(FX, row)
            at.put(FACE_Y, row, masked(value, row))
        if FACE_Z in names:
            value = at(FX, row) - at.fy(FX, row) + at.fx(FY, row) - at(FY, row)
            at.put(FACE_Z, row, masked(value, row))
        if COEF in names:
            diag = 3.0 * at(SX, row) + at.bx(SX, row) + at.by(SX, row) + at.bz(SX, row)
            at.put(COEF, row, over(OMEGA_NODE, diag, row))
        if Q_Y in names:
            at.put(Q_Y, row, at(FY, row) * scale(at(SX, row)))

    def residual_pass(at, row, names):
        g = scale(at(SX, row))
        if RES_X in names:
            z, y = at(FACE_Z, row), at(FACE_Y, row)
            edge = z - at.by(FACE_Z, row) - y + at.bz(FACE_Y, row)
            at.put(RES_X, row, at(FX, row) * g - edge)
        if RES_Y in names:
            z, x = at(FACE_Z, row), at(FACE_X, row)
            edge = at.bx(FACE_Z, row) - z + x - at.bz(FACE_X, row)
            at.put(RES_Y, row, at(Q_Y, row) - edge)
        if RES_Z in names:
            x, y = at(FACE_X, row), at(FACE_Y, row)
            edge = at.by(FACE_X, row) - x + y - at.bx(FACE_Y, row)
            at.put(RES_Z, row, at(FZ, row) * g - edge)
        if NODE in names:
            q_x = at(FX, row) * g
            if row is strip:
                back_x = turn(q_x, COLS)
            else:
                back_x = at(FX, row - 1) * scale(at(SX, row - 1))
            back_z = at.bz(FZ, row) * scale(at.bz(SX, row))
            change_y = at.by(Q_Y, row) - at(Q_Y, row)
            at.put(NODE, row, back_x - q_x + change_y + back_z - at(FZ, row) * g)
        if PHI in names:
            at.put(PHI, row, at(COEF, row) * at(NODE, row))

    def flow_pass(at, row, names):
        if FLOW_Y in names:
            at.put(FLOW_Y, row, at(SX, row) * (at.fy(PHI, row) - at(PHI, row)))
        if row is strip:
            const_x, const_y = strip_back_x, strip_back_y
        else:
            const_y = main_back_y
            const_x = 4.0 + 4.0 * has_low if row in (-1, 0) else 8.0
        const_z = jnp.where(level == 0, 4.0, 8.0).astype(F32) if at.base == 0 else 8.0
        for f, (const, back) in enumerate(((const_x, at.bx), (const_y, at.by), (const_z, at.bz))):
            if PSI_X + f in names:
                total = at(SX, row) + back(SX, row) + const
                value = at(RES_X + f, row) + back(RES_X + f, row)
                at.put(PSI_X + f, row, over(value, total, row))

    def middle_pass(at, row, names):
        if PHI2 in names:
            sigma, phi = at(SX, row), at(PHI, row)
            flow_x = sigma * (at.fx(PHI, row) - phi)
            back_x = at.bx(SX, row) * (phi - at.bx(PHI, row))
            flow_z = sigma * (at.fz(PHI, row) - phi)
            back_z = at.bz(SX, row) * (phi - at.bz(PHI, row))
            change_y = at.by(FLOW_Y, row) - at(FLOW_Y, row)
            applied = back_x - flow_x + change_y + back_z - flow_z
            at.put(PHI2, row, phi + at(COEF, row) * (at(NODE, row) - applied))
        for f, ahead in enumerate((at.fx, at.fy, at.fz)):
            if MID_X + f in names:
                at.put(MID_X + f, row, 0.5 * (at(PSI_X + f, row) + ahead(PSI_X + f, row)))

    def turn_pass(at, row, names):
        if TURN_X in names:
            value = at(MID_Y, row) - at.fz(MID_Y, row) + at.fy(MID_Z, row) - at(MID_Z, row)
            at.put(TURN_X, row, masked(value, row))
        if TURN_Y in names:
            value = at(MID_Z, row) - at.fx(MID_Z, row) + at.fz(MID_X, row) - at(MID_X, row)
            at.put(TURN_Y, row, masked(value, row))
        if TURN_Z in names:
            value = at(MID_X, row) - at.fy(MID_X, row) + at.fx(MID_Y, row) - at(MID_Y, row)
            at.put(TURN_Z, row, masked(value, row))

    def last_pass(at, row, names):
        sigma, phi = at(SX, row), at(PHI2, row)
        x, y, z = at(TURN_X, row), at(TURN_Y, row), at(TURN_Z, row)
        edges = (
            z - at.by(TURN_Z, row) - y + at.bz(TURN_Y, row),
            at.bx(TURN_Z, row) - z + x - at.bz(TURN_X, row),
            at.by(TURN_X, row) - x + y - at.bx(TURN_Y, row),
        )
        for f, ahead in enumerate((at.fx, at.fy, at.fz)):
            change = ahead(PHI2, row) - phi + at(MID_X + f, row)
            final = at(RES_X + f, row) - edges[f] - sigma * change
            emit(at.base, row, f, at(FX + f, row) + change, final)

    steps = (first_pass, face_pass, residual_pass, flow_pass, middle_pass, turn_pass, last_pass)
    for names, step in zip(PASSES, steps):
        wanted = [item for item in todo if item[0] in names]
        rows_now = ([] if step is last_pass else [strip]) + sorted({row for _, row in wanted})
        for row in rows_now:
            here = names if row is strip else [name for name in names if (name, row) in wanted]
            for base in range(0, depth, TILE):
                if step is not last_pass:
                    step(At(base), row, here)
    for base in range(0, depth, TILE):
        for row in sorted(row for name, row in todo if name == OUT):
            last_pass(At(base), row, (OUT,))
        if leave is not None:
            leave(base)


def strip_reader(cells_x, place, own, got_a, got_b, corner_a, corner_b):
    lane = lanes()
    rows = cells_x + 2 * REACH
    row = jnp.clip(lane // COLS - REACH, 0, cells_x - 1)
    column = lane % COLS
    index = [strip_index(cells_x, f, row, column) for f in range(4)]
    even_x, even_y = place[0] % 2 == 0, place[1] % 2 == 0
    per_field = LANES // 4
    far = (rows - REACH) * COLS

    def strips(base):
        where = pl.ds(base, TILE)
        mine, a, b = own[where, :], got_a[where, :], got_b[where, :]
        left, right = jnp.where(even_y, b, a), jnp.where(even_y, a, b)
        if corner_a is not None:
            a, b = corner_a[where, :], corner_b[where, :]
            low, high = jnp.where(even_x, b, a), jnp.where(even_x, a, b)
        values = []
        for f in range(4):
            v = strip_source(column, pick(mine, index[f]), pick(left, index[f]), pick(right, index[f]))
            v = jnp.where((lane < REACH * COLS) | (lane >= far), 0.0, v)
            if corner_a is not None:
                moved = turn(low, -(f * per_field + REACH * COLS))
                v = jnp.where(lane < REACH * COLS, moved, v)
                moved = turn(high, far - f * per_field)
                v = jnp.where((lane >= far) & (lane < rows * COLS), moved, v)
            values.append(v)
        return values

    return strips


def writer(cells_x, corrected, final):
    def emit(base, row, f, value, rest):
        where = pl.ds(base * cells_x + row, TILE, stride=cells_x)
        corrected[f, where, :] = value
        final[f, where, :] = rest

    return emit


def early_rows(
    plan,
    sizes,
    place,
    table,
    held,
    own,
    got_a,
    got_b,
    rows_a,
    rows_b,
    kept,
    corrected,
    final,
    scratch,
    strip_ref,
):
    cells_x = plan.cells_x

    def fetch(base, row):
        return [held[f, row, pl.ds(base, TILE), :] for f in range(4)]

    strips = strip_reader(cells_x, place, own, got_a, got_b, None, None)
    slots = {item: (kept, i) for i, item in enumerate(plan.kept)}
    others = [item for item in plan.early if item not in slots and item[0] != OUT]
    slots |= {item: (scratch, i) for i, item in enumerate(others)}
    table = table[...]
    emit = writer(cells_x, corrected, final)
    run_cycle(plan, False, sizes, place, table, fetch, strips, slots, strip_ref, emit, own.shape[0])


def late_rows(
    plan,
    sizes,
    place,
    table,
    own,
    got_a,
    got_b,
    rows_a,
    corner_a,
    rows_b,
    corner_b,
    kept,
    _part_corrected,
    _part_final,
    corrected,
    final,
    part_corrected,
    part_final,
    scratch,
    strip_ref,
    sems,
):
    cells_x = plan.cells_x
    even = place[0] % 2 == 0
    depth = own.shape[0]
    copies = []

    def leave(base):
        step = depth // RUNS
        if (base + TILE) % step == 0:
            where = pl.ds((base + TILE - step) * cells_x, step * cells_x)
            for source, target in ((part_corrected, corrected), (part_final, final)):
                copy = pltpu.make_async_copy(
                    source.at[:, where, :], target.at[:, where, :], sems.at[len(copies)]
                )
                copy.start()
                copies.append(copy)

    def fetch(base, row):
        first = (row + REACH if row < 0 else row - cells_x) * 4
        values = []
        for f in range(4):
            a, b = (ref[first + f, pl.ds(base, TILE), :] for ref in (rows_a, rows_b))
            values.append(jnp.where(even, b, a) if row < 0 else jnp.where(even, a, b))
        return values

    strips = strip_reader(cells_x, place, own, got_a, got_b, corner_a, corner_b)
    slots = {item: (kept, i) for i, item in enumerate(plan.kept)}
    others = [item for item in plan.late if item[0] != OUT]
    slots |= {item: (scratch, i) for i, item in enumerate(others)}
    table = table[...]
    emit = writer(cells_x, part_corrected, part_final)
    run_cycle(plan, True, sizes, place, table, fetch, strips, slots, strip_ref, emit, depth, leave)
    for copy in copies:
        copy.wait()


def swaps(count, first):
    pairs = [(i, i + 1) for i in range(first, count - 1, 2)]
    return pairs + [(j, i) for i, j in pairs]


def local(right_side, material, conductivity):
    depth, cells_x, cells_y = material.shape
    size_x, size_y = lax.axis_size("gx"), lax.axis_size("gy")
    place = jnp.stack([lax.axis_index("gx"), lax.axis_index("gy")]).astype(jnp.int32)
    table = class_table(conductivity)
    source = right_side.reshape(3, depth * cells_x, cells_y)
    classes = material.reshape(depth * cells_x, cells_y)
    vmem = pl.BlockSpec(memory_space=pltpu.VMEM)
    hbm = pl.BlockSpec(memory_space=pltpu.HBM)
    smem = pl.BlockSpec(memory_space=pltpu.SMEM)
    slab = jax.ShapeDtypeStruct((depth, cells_y), F32)

    def slabs(count):
        return jax.ShapeDtypeStruct((count, depth, cells_y), F32)

    def padded(count):
        return (count, depth + 2 * PAD, cells_y)

    def params(mib):
        return pltpu.CompilerParams(vmem_limit_bytes=mib * 2**20)

    outs = (
        slab,
        slabs(4 * REACH),
        slabs(4 * REACH),
        jax.ShapeDtypeStruct((4, cells_x, depth, cells_y), F32),
    )
    outs = pl.pallas_call(
        functools.partial(gather_classes, cells_x),
        out_shape=outs,
        in_specs=[smem, vmem],
        out_specs=(vmem,) * 4,
        compiler_params=params(16),
        cost_estimate=pl.CostEstimate(flops=10**9, bytes_accessed=1000, transcendentals=0),
        name="gather_classes",
    )(place, classes)
    own, rows_a, rows_b, held = pl.pallas_call(
        functools.partial(gather_source, cells_x),
        out_shape=tuple(jax.ShapeDtypeStruct(out.shape, F32) for out in outs),
        in_specs=[smem] + [vmem] * 5,
        out_specs=(vmem,) * 4,
        input_output_aliases={2: 0, 3: 1, 4: 2, 5: 3},
        compiler_params=params(16),
        name="gather_source",
    )(place, source, *outs)
    got_b = lax.ppermute(own, "gy", swaps(size_y, 1))
    got_a = lax.ppermute(own, "gy", swaps(size_y, 0))
    corners = pl.pallas_call(
        functools.partial(corner_strips, cells_x),
        out_shape=slab,
        in_specs=[smem] + [vmem] * 3,
        out_specs=vmem,
        compiler_params=params(16),
        name="corner_strips",
    )(place, own, got_a, got_b)
    corner_b = lax.ppermute(corners, "gx", swaps(size_x, 1))
    corner_a = lax.ppermute(corners, "gx", swaps(size_x, 0))
    rows_b = lax.ppermute(rows_b, "gx", swaps(size_x, 1))
    rows_a = lax.ppermute(rows_a, "gx", swaps(size_x, 0))

    plan, sizes = Plan(cells_x), (size_x, size_y)
    flat = jax.ShapeDtypeStruct(source.shape, F32)
    strip_shape = pltpu.VMEM(padded(COUNT), F32)
    kept, corrected, final = pl.pallas_call(
        functools.partial(early_rows, plan, sizes),
        out_shape=(jax.ShapeDtypeStruct(padded(len(plan.kept)), F32), flat, flat),
        in_specs=[smem] + [vmem] * 7,
        out_specs=(vmem, vmem, vmem),
        scratch_shapes=[pltpu.VMEM(padded(len(plan.early)), F32), strip_shape],
        compiler_params=params(32),
        cost_estimate=pl.CostEstimate(flops=EARLY_FLOPS, bytes_accessed=0, transcendentals=0),
        name="early_rows",
    )(place, table, held, own, got_a, got_b, rows_a, rows_b)
    corrected, final, _, _ = pl.pallas_call(
        functools.partial(late_rows, plan, sizes),
        out_shape=(flat,) * 4,
        in_specs=[smem] + [vmem] * 11,
        out_specs=(hbm, hbm, vmem, vmem),
        input_output_aliases={10: 2, 11: 3},
        scratch_shapes=[
            pltpu.VMEM(padded(len(plan.late)), F32),
            strip_shape,
            pltpu.SemaphoreType.DMA((2 * RUNS,)),
        ],
        compiler_params=params(32),
        name="late_rows",
    )(place, table, own, got_a, got_b, rows_a, corner_a, rows_b, corner_b, kept, corrected, final)
    return corrected.reshape(right_side.shape), final.reshape(right_side.shape)


def solution(mesh):
    return jax.shard_map(
        local,
        mesh=mesh,
        in_specs=(P(None, None, "gx", "gy"), P(None, "gx", "gy"), P()),
        out_specs=(P(None, None, "gx", "gy"), P(None, None, "gx", "gy")),
        check_vma=False,
    )
```

```python
import functools

import jax
import jax.numpy as jnp
from jax import lax
from jax.experimental import pallas as pl
from jax.experimental.pallas import tpu as pltpu
from jax.sharding import PartitionSpec as P

OMEGA_EDGE = 0.6
OMEGA_NODE = 0.7
F32 = jnp.float32
LANES = 128
TILE = 8
REACH = 2
WIDE = 2 * REACH
COLS = 2 * WIDE
EARLY_FLOPS = 10**10
RUNS = 4
PAD = 8


def lanes():
    return lax.broadcasted_iota(jnp.int32, (TILE, LANES), 1)


def class_table(conductivity):
    row = jnp.pad(conductivity, (1, LANES - 1 - conductivity.shape[0]))
    return jnp.broadcast_to(row[None], (TILE, LANES))


def pick(table, index):
    return jnp.take_along_axis(table, index, axis=1)


def turn(value, amount):
    amount = amount % LANES
    return value if amount == 0 else pltpu.roll(value, amount, 1)


def code(material):
    return (material + 1).astype(F32)


def gather(cells_x, place, fields, load, merge, edges, rows_a, rows_b, held):
    depth = edges.shape[0]
    lane = lanes()
    even = place[0] % 2 == 0
    row_a = jnp.where(even, cells_x - REACH, 0)
    row_b = jnp.where(even, 0, cells_x - REACH)
    for base in range(0, depth, TILE):
        where = pl.ds(base, TILE)
        packed = edges[where, :] if merge else jnp.zeros((TILE, LANES), F32)
        for field in fields:
            for row in range(cells_x):
                slot = (field * cells_x + row) * WIDE
                value = load(field, base, row)
                held[field, row, where, :] = value
                value = turn(value, slot + REACH)
                packed = jnp.where((lane >= slot) & (lane < slot + WIDE), value, packed)
            for out, first in ((rows_a, row_a), (rows_b, row_b)):
                for row in range(REACH):
                    out[row * 4 + field, where, :] = load(field, base, first + row)
        edges[where, :] = packed


def gather_classes(cells_x, place, material, edges, *outs):
    def load(field, base, row):
        return code(material[pl.ds(base * cells_x + row, TILE, stride=cells_x), :])

    gather(cells_x, place, (3,), load, False, edges, *outs)


def gather_source(cells_x, place, source, _edges, _rows_a, _rows_b, _held, edges, *outs):
    def load(field, base, row):
        return source[field, pl.ds(base * cells_x + row, TILE, stride=cells_x), :]

    gather(cells_x, place, range(3), load, True, edges, *outs)


def strip_index(cells_x, field, row, column):
    return (field * cells_x + row) * WIDE + column % WIDE


def strip_source(column, own, left, right):
    return jnp.where(column < REACH, left, jnp.where(column < COLS - REACH, own, right))


def corner_strips(cells_x, place, own, got_a, got_b, out):
    depth = own.shape[0]
    lane = lanes()
    per_field = LANES // 4
    field, rank, column = lane // per_field, (lane % per_field) // COLS, lane % COLS
    row = jnp.where(rank < REACH, rank, cells_x - 2 * REACH + rank)
    index = strip_index(cells_x, field, row, column)
    even = place[1] % 2 == 0
    for base in range(0, depth, TILE):
        where = pl.ds(base, TILE)
        mine, a, b = (pick(ref[where, :], index) for ref in (own, got_a, got_b))
        left, right = jnp.where(even, b, a), jnp.where(even, a, b)
        out[where, :] = strip_source(column, mine, left, right)


(SX, FX, FY, FZ, FACE_X, FACE_Y, FACE_Z, COEF, Q_Y) = range(9)
(RES_X, RES_Y, RES_Z, NODE, PHI, FLOW_Y, PSI_X, PSI_Y, PSI_Z) = range(9, 18)
(PHI2, MID_X, MID_Y, MID_Z, TURN_X, TURN_Y, TURN_Z, OUT) = range(18, 26)
COUNT = OUT

READS = {
    SX: (),
    FX: (),
    FY: (),
    FZ: (),
    FACE_X: ((FY, 0), (FZ, 0)),
    FACE_Y: ((FZ, 0), (FZ, 1), (FX, 0)),
    FACE_Z: ((FX, 0), (FY, 0), (FY, 1)),
    COEF: ((SX, 0), (SX, -1)),
    Q_Y: ((FY, 0), (SX, 0)),
    RES_X: ((FX, 0), (SX, 0), (FACE_Z, 0), (FACE_Y, 0)),
    RES_Y: ((Q_Y, 0), (FACE_Z, -1), (FACE_Z, 0), (FACE_X, 0)),
    RES_Z: ((FZ, 0), (SX, 0), (FACE_X, 0), (FACE_Y, 0), (FACE_Y, -1)),
    NODE: ((FX, 0), (SX, 0), (FX, -1), (SX, -1), (Q_Y, 0), (FZ, 0)),
    PHI: ((COEF, 0), (NODE, 0)),
    FLOW_Y: ((SX, 0), (PHI, 0)),
    PSI_X: ((RES_X, 0), (RES_X, -1), (SX, 0), (SX, -1)),
    PSI_Y: ((RES_Y, 0), (SX, 0)),
    PSI_Z: ((RES_Z, 0), (SX, 0)),
    PHI2: (
        (SX, 0),
        (SX, -1),
        (PHI, 0),
        (PHI, 1),
        (PHI, -1),
        (FLOW_Y, 0),
        (COEF, 0),
        (NODE, 0),
    ),
    MID_X: ((PSI_X, 0), (PSI_X, 1)),
    MID_Y: ((PSI_Y, 0),),
    MID_Z: ((PSI_Z, 0),),
    TURN_X: ((MID_Y, 0), (MID_Z, 0)),
    TURN_Y: ((MID_Z, 0), (MID_Z, 1), (MID_X, 0)),
    TURN_Z: ((MID_X, 0), (MID_Y, 0), (MID_Y, 1)),
    OUT: (
        (TURN_X, 0),
        (TURN_Y, 0),
        (TURN_Y, -1),
        (TURN_Z, 0),
        (TURN_Z, -1),
        (PHI2, 0),
        (PHI2, 1),
        (MID_X, 0),
        (MID_Y, 0),
        (MID_Z, 0),
        (FX, 0),
        (FY, 0),
        (FZ, 0),
        (SX, 0),
        (RES_X, 0),
        (RES_Y, 0),
        (RES_Z, 0),
    ),
}
Z_READ = (SX, FX, FY, FZ, FACE_X, FACE_Y, RES_Z, PHI)
Z_READ += (PHI2, PSI_Z, MID_X, MID_Y, TURN_X, TURN_Y)
PASSES = (
    (SX, FX, FY, FZ),
    (FACE_X, FACE_Y, FACE_Z, COEF, Q_Y),
    (RES_X, RES_Y, RES_Z, NODE, PHI),
    (FLOW_Y, PSI_X, PSI_Y, PSI_Z),
    (PHI2, MID_X, MID_Y, MID_Z),
    (TURN_X, TURN_Y, TURN_Z),
    (OUT,),
)


class Plan:
    def __init__(self, cells_x):
        self.cells_x = cells_x
        need = {(OUT, row) for row in range(cells_x)}
        todo = list(need)
        while todo:
            name, row = todo.pop()
            for read, offset in READS[name]:
                if (read, row + offset) not in need:
                    need.add((read, row + offset))
                    todo.append((read, row + offset))

        def early(name, row):
            if not READS[name]:
                return 0 <= row < cells_x
            return all(early(read, row + offset) for read, offset in READS[name])

        need = sorted(need)
        self.early = [item for item in need if early(*item)]
        self.late = [item for item in need if not early(*item)]
        used = {(read, row + offset) for name, row in self.late for read, offset in READS[name]}
        self.kept = [item for item in self.early if item in used]


def run_cycle(plan, late, sizes, place, table, fetch, strips, slots, strip_ref, emit, depth, leave=None):
    cells_x = plan.cells_x
    rows = cells_x + 2 * REACH
    lane = lanes()
    level = lax.broadcasted_iota(jnp.int32, (TILE, LANES), 0)
    has_low = jnp.where(place[0] > 0, 1.0, 0.0).astype(F32)
    has_high = jnp.where(place[0] < sizes[0] - 1, 1.0, 0.0).astype(F32)
    first_col = jnp.where(place[1] > 0, 4.0, 0.0).astype(F32)
    todo = plan.late if late else plan.early
    strip = None

    zeros = jnp.zeros((PAD, LANES), F32)
    for name, row in todo:
        if name in Z_READ:
            ref, slot = slots[name, row]
            ref[slot, pl.ds(0, PAD), :] = zeros
            ref[slot, pl.ds(PAD + depth, PAD), :] = zeros
    for name in Z_READ:
        strip_ref[name, pl.ds(0, PAD), :] = zeros
        strip_ref[name, pl.ds(PAD + depth, PAD), :] = zeros

    strip_row = lane // COLS - REACH
    column = lane % COLS
    strip_col = jnp.where(column < WIDE, column - REACH, column - WIDE - REACH + LANES)

    def inside(index, axis, length):
        at = index + place[axis] * length
        return (at >= 0) & (at < sizes[axis] * length)

    held = lane < rows * COLS
    if not late:
        held &= (strip_row >= 0) & (strip_row < cells_x)
    in_x, in_y = inside(strip_row, 0, cells_x), inside(strip_col, 1, LANES)
    strip_mask = jnp.where(in_x & in_y & held, 1.0, 0.0).astype(F32)
    strip_back_x = jnp.where(inside(strip_row - 1, 0, cells_x), 8.0, 4.0).astype(F32)
    strip_back_y = jnp.where(inside(strip_col - 1, 1, LANES), 8.0, 4.0).astype(F32)
    main_back_y = 4.0 + jnp.where(lane == 0, first_col, 4.0).astype(F32)

    def mask(row):
        if row is strip:
            return strip_mask
        if row < 0:
            return has_low
        return has_high if row >= cells_x else None

    def masked(value, row):
        m = mask(row)
        return value if m is None else value * m

    def over(top, bottom, row):
        m = mask(row)
        return top / bottom if m is None else (top * m) / (bottom + (1.0 - m))

    def scale(sigma):
        return sigma * (2.0 / 3.0) + 20.0 / 3.0

    class At:
        def __init__(self, base):
            self.base = base
            self.seen = {}

        def where(self, name, row, dz=0):
            ref, slot = (strip_ref, name) if row is strip else slots[name, row]
            return ref, slot, pl.ds(self.base + PAD + dz, TILE)

        def __call__(self, name, row, dz=0):
            key = (name, row, dz)
            if key not in self.seen:
                ref, slot, rows_z = self.where(name, row, dz)
                self.seen[key] = ref[slot, rows_z, :]
            return self.seen[key]

        def put(self, name, row, value):
            ref, slot, rows_z = self.where(name, row)
            ref[slot, rows_z, :] = value
            self.seen[name, row, 0] = value

        def fz(self, name, row):
            return self(name, row, 1)

        def bz(self, name, row):
            return self(name, row, -1)

        def fx(self, name, row):
            return turn(self(name, row), -COLS) if row is strip else self(name, row + 1)

        def bx(self, name, row):
            return turn(self(name, row), COLS) if row is strip else self(name, row - 1)

        def fy(self, name, row):
            moved = turn(self(name, row), -1)
            if row is strip:
                return moved
            start = (row + REACH) * COLS + COLS - REACH
            edge = turn(self(name, strip), LANES - 1 - start)
            return jnp.where(lane == LANES - 1, edge, moved)

        def by(self, name, row):
            moved = turn(self(name, row), 1)
            if row is strip:
                return moved
            edge = turn(self(name, strip), -((row + REACH) * COLS + REACH - 1))
            return jnp.where(lane == 0, edge, moved)

    def first_pass(at, row, names):
        x, y, z, codes = strips(at.base) if row is strip else fetch(at.base, row)
        sigma = pick(table, codes.astype(jnp.int32))
        weight = OMEGA_EDGE / (4.0 + sigma)
        for name, value in ((SX, sigma), (FX, x * weight), (FY, y * weight), (FZ, z * weight)):
            if name in names:
                at.put(name, row, value)

    def face_pass(at, row, names):
        if FACE_X in names:
            value = at(FY, row) - at.fz(FY, row) + at.fy(FZ, row) - at(FZ, row)
            at.put(FACE_X, row, masked(value, row))
        if FACE_Y in names:
            value = at(FZ, row) - at.fx(FZ, row) + at.fz(FX, row) - at(FX, row)
            at.put(FACE_Y, row, masked(value, row))
        if FACE_Z in names:
            value = at(FX, row) - at.fy(FX, row) + at.fx(FY, row) - at(FY, row)
            at.put(FACE_Z, row, masked(value, row))
        if COEF in names:
            diag = 3.0 * at(SX, row) + at.bx(SX, row) + at.by(SX, row) + at.bz(SX, row)
            at.put(COEF, row, over(OMEGA_NODE, diag, row))
        if Q_Y in names:
            at.put(Q_Y, row, at(FY, row) * scale(at(SX, row)))

    def residual_pass(at, row, names):
        g = scale(at(SX, row))
        if RES_X in names:
            z, y = at(FACE_Z, row), at(FACE_Y, row)
            edge = z - at.by(FACE_Z, row) - y + at.bz(FACE_Y, row)
            at.put(RES_X, row, at(FX, row) * g - edge)
        if RES_Y in names:
            z, x = at(FACE_Z, row), at(FACE_X, row)
            edge = at.bx(FACE_Z, row) - z + x - at.bz(FACE_X, row)
            at.put(RES_Y, row, at(Q_Y, row) - edge)
        if RES_Z in names:
            x, y = at(FACE_X, row), at(FACE_Y, row)
            edge = at.by(FACE_X, row) - x + y - at.bx(FACE_Y, row)
            at.put(RES_Z, row, at(FZ, row) * g - edge)
        if NODE in names:
            q_x = at(FX, row) * g
            if row is strip:
                back_x = turn(q_x, COLS)
            else:
                back_x = at(FX, row - 1) * scale(at(SX, row - 1))
            back_z = at.bz(FZ, row) * scale(at.bz(SX, row))
            change_y = at.by(Q_Y, row) - at(Q_Y, row)
            at.put(NODE, row, back_x - q_x + change_y + back_z - at(FZ, row) * g)
        if PHI in names:
            at.put(PHI, row, at(COEF, row) * at(NODE, row))

    def flow_pass(at, row, names):
        if FLOW_Y in names:
            at.put(FLOW_Y, row, at(SX, row) * (at.fy(PHI, row) - at(PHI, row)))
        if row is strip:
            const_x, const_y = strip_back_x, strip_back_y
        else:
            const_y = main_back_y
            const_x = 4.0 + 4.0 * has_low if row in (-1, 0) else 8.0
        const_z = jnp.where(level == 0, 4.0, 8.0).astype(F32) if at.base == 0 else 8.0
        for f, (const, back) in enumerate(((const_x, at.bx), (const_y, at.by), (const_z, at.bz))):
            if PSI_X + f in names:
                total = at(SX, row) + back(SX, row) + const
                value = at(RES_X + f, row) + back(RES_X + f, row)
                at.put(PSI_X + f, row, over(value, total, row))

    def middle_pass(at, row, names):
        if PHI2 in names:
            sigma, phi = at(SX, row), at(PHI, row)
            flow_x = sigma * (at.fx(PHI, row) - phi)
            back_x = at.bx(SX, row) * (phi - at.bx(PHI, row))
            flow_z = sigma * (at.fz(PHI, row) - phi)
            back_z = at.bz(SX, row) * (phi - at.bz(PHI, row))
            change_y = at.by(FLOW_Y, row) - at(FLOW_Y, row)
            applied = back_x - flow_x + change_y + back_z - flow_z
            at.put(PHI2, row, phi + at(COEF, row) * (at(NODE, row) - applied))
        for f, ahead in enumerate((at.fx, at.fy, at.fz)):
            if MID_X + f in names:
                at.put(MID_X + f, row, 0.5 * (at(PSI_X + f, row) + ahead(PSI_X + f, row)))

    def turn_pass(at, row, names):
        if TURN_X in names:
            value = at(MID_Y, row) - at.fz(MID_Y, row) + at.fy(MID_Z, row) - at(MID_Z, row)
            at.put(TURN_X, row, masked(value, row))
        if TURN_Y in names:
            value = at(MID_Z, row) - at.fx(MID_Z, row) + at.fz(MID_X, row) - at(MID_X, row)
            at.put(TURN_Y, row, masked(value, row))
        if TURN_Z in names:
            value = at(MID_X, row) - at.fy(MID_X, row) + at.fx(MID_Y, row) - at(MID_Y, row)
            at.put(TURN_Z, row, masked(value, row))

    def last_pass(at, row, names):
        sigma, phi = at(SX, row), at(PHI2, row)
        x, y, z = at(TURN_X, row), at(TURN_Y, row), at(TURN_Z, row)
        edges = (
            z - at.by(TURN_Z, row) - y + at.bz(TURN_Y, row),
            at.bx(TURN_Z, row) - z + x - at.bz(TURN_X, row),
            at.by(TURN_X, row) - x + y - at.bx(TURN_Y, row),
        )
        for f, ahead in enumerate((at.fx, at.fy, at.fz)):
            change = ahead(PHI2, row) - phi + at(MID_X + f, row)
            final = at(RES_X + f, row) - edges[f] - sigma * change
            emit(at.base, row, f, at(FX + f, row) + change, final)

    steps = (first_pass, face_pass, residual_pass, flow_pass, middle_pass, turn_pass, last_pass)
    for names, step in zip(PASSES, steps):
        wanted = [item for item in todo if item[0] in names]
        rows_now = ([] if step is last_pass else [strip]) + sorted({row for _, row in wanted})
        for row in rows_now:
            here = names if row is strip else [name for name in names if (name, row) in wanted]
            for base in range(0, depth, TILE):
                if step is not last_pass:
                    step(At(base), row, here)
    for base in range(0, depth, TILE):
        for row in sorted(row for name, row in todo if name == OUT):
            last_pass(At(base), row, (OUT,))
        if leave is not None:
            leave(base)


def strip_reader(cells_x, place, own, got_a, got_b, corner_a, corner_b):
    lane = lanes()
    rows = cells_x + 2 * REACH
    row = jnp.clip(lane // COLS - REACH, 0, cells_x - 1)
    column = lane % COLS
    index = [strip_index(cells_x, f, row, column) for f in range(4)]
    even_x, even_y = place[0] % 2 == 0, place[1] % 2 == 0
    per_field = LANES // 4
    far = (rows - REACH) * COLS

    def strips(base):
        where = pl.ds(base, TILE)
        mine, a, b = own[where, :], got_a[where, :], got_b[where, :]
        left, right = jnp.where(even_y, b, a), jnp.where(even_y, a, b)
        if corner_a is not None:
            a, b = corner_a[where, :], corner_b[where, :]
            low, high = jnp.where(even_x, b, a), jnp.where(even_x, a, b)
        values = []
        for f in range(4):
            v = strip_source(column, pick(mine, index[f]), pick(left, index[f]), pick(right, index[f]))
            v = jnp.where((lane < REACH * COLS) | (lane >= far), 0.0, v)
            if corner_a is not None:
                moved = turn(low, -(f * per_field + REACH * COLS))
                v = jnp.where(lane < REACH * COLS, moved, v)
                moved = turn(high, far - f * per_field)
                v = jnp.where((lane >= far) & (lane < rows * COLS), moved, v)
            values.append(v)
        return values

    return strips


def writer(cells_x, corrected, final):
    def emit(base, row, f, value, rest):
        where = pl.ds(base * cells_x + row, TILE, stride=cells_x)
        corrected[f, where, :] = value
        final[f, where, :] = rest

    return emit


def early_rows(
    plan,
    sizes,
    place,
    table,
    held,
    own,
    got_a,
    got_b,
    rows_a,
    kept,
    corrected,
    final,
    scratch,
    strip_ref,
):
    cells_x = plan.cells_x

    def fetch(base, row):
        return [held[f, row, pl.ds(base, TILE), :] for f in range(4)]

    strips = strip_reader(cells_x, place, own, got_a, got_b, None, None)
    slots = {item: (kept, i) for i, item in enumerate(plan.kept)}
    others = [item for item in plan.early if item not in slots and item[0] != OUT]
    slots |= {item: (scratch, i) for i, item in enumerate(others)}
    table = table[...]
    emit = writer(cells_x, corrected, final)
    run_cycle(plan, False, sizes, place, table, fetch, strips, slots, strip_ref, emit, own.shape[0])


def late_rows(
    plan,
    sizes,
    place,
    table,
    own,
    got_a,
    got_b,
    rows_a,
    corner_a,
    rows_b,
    corner_b,
    kept,
    _part_corrected,
    _part_final,
    corrected,
    final,
    part_corrected,
    part_final,
    scratch,
    strip_ref,
    sems,
):
    cells_x = plan.cells_x
    even = place[0] % 2 == 0
    depth = own.shape[0]
    copies = []

    def leave(base):
        step = depth // RUNS
        if (base + TILE) % step == 0:
            where = pl.ds((base + TILE - step) * cells_x, step * cells_x)
            for source, target in ((part_corrected, corrected), (part_final, final)):
                copy = pltpu.make_async_copy(
                    source.at[:, where, :], target.at[:, where, :], sems.at[len(copies)]
                )
                copy.start()
                copies.append(copy)

    def fetch(base, row):
        first = (row + REACH if row < 0 else row - cells_x) * 4
        values = []
        for f in range(4):
            a, b = (ref[first + f, pl.ds(base, TILE), :] for ref in (rows_a, rows_b))
            values.append(jnp.where(even, b, a) if row < 0 else jnp.where(even, a, b))
        return values

    strips = strip_reader(cells_x, place, own, got_a, got_b, corner_a, corner_b)
    slots = {item: (kept, i) for i, item in enumerate(plan.kept)}
    others = [item for item in plan.late if item[0] != OUT]
    slots |= {item: (scratch, i) for i, item in enumerate(others)}
    table = table[...]
    emit = writer(cells_x, part_corrected, part_final)
    run_cycle(plan, True, sizes, place, table, fetch, strips, slots, strip_ref, emit, depth, leave)
    for copy in copies:
        copy.wait()


def swaps(count, first):
    pairs = [(i, i + 1) for i in range(first, count - 1, 2)]
    return pairs + [(j, i) for i, j in pairs]


def local(right_side, material, conductivity):
    depth, cells_x, cells_y = material.shape
    size_x, size_y = lax.axis_size("gx"), lax.axis_size("gy")
    place = jnp.stack([lax.axis_index("gx"), lax.axis_index("gy")]).astype(jnp.int32)
    table = class_table(conductivity)
    source = right_side.reshape(3, depth * cells_x, cells_y)
    classes = material.reshape(depth * cells_x, cells_y)
    vmem = pl.BlockSpec(memory_space=pltpu.VMEM)
    hbm = pl.BlockSpec(memory_space=pltpu.HBM)
    smem = pl.BlockSpec(memory_space=pltpu.SMEM)
    slab = jax.ShapeDtypeStruct((depth, cells_y), F32)

    def slabs(count):
        return jax.ShapeDtypeStruct((count, depth, cells_y), F32)

    def padded(count):
        return (count, depth + 2 * PAD, cells_y)

    def params(mib):
        return pltpu.CompilerParams(vmem_limit_bytes=mib * 2**20)

    outs = (
        slab,
        slabs(4 * REACH),
        slabs(4 * REACH),
        jax.ShapeDtypeStruct((4, cells_x, depth, cells_y), F32),
    )
    outs = pl.pallas_call(
        functools.partial(gather_classes, cells_x),
        out_shape=outs,
        in_specs=[smem, vmem],
        out_specs=(vmem,) * 4,
        compiler_params=params(16),
        cost_estimate=pl.CostEstimate(flops=10**9, bytes_accessed=1000, transcendentals=0),
        name="gather_classes",
    )(place, classes)
    own, rows_a, rows_b, held = pl.pallas_call(
        functools.partial(gather_source, cells_x),
        out_shape=tuple(jax.ShapeDtypeStruct(out.shape, F32) for out in outs),
        in_specs=[smem] + [vmem] * 5,
        out_specs=(vmem,) * 4,
        input_output_aliases={2: 0, 3: 1, 4: 2, 5: 3},
        compiler_params=params(16),
        name="gather_source",
    )(place, source, *outs)
    got_b = lax.ppermute(own, "gy", swaps(size_y, 1))
    got_a = lax.ppermute(own, "gy", swaps(size_y, 0))
    corners = pl.pallas_call(
        functools.partial(corner_strips, cells_x),
        out_shape=slab,
        in_specs=[smem] + [vmem] * 3,
        out_specs=vmem,
        compiler_params=params(16),
        name="corner_strips",
    )(place, own, got_a, got_b)
    corner_a = lax.ppermute(corners, "gx", swaps(size_x, 0))
    corner_b = lax.ppermute(corners, "gx", swaps(size_x, 1))
    rows_b = lax.ppermute(rows_b, "gx", swaps(size_x, 1))
    rows_a = lax.ppermute(rows_a, "gx", swaps(size_x, 0))

    plan, sizes = Plan(cells_x), (size_x, size_y)
    flat = jax.ShapeDtypeStruct(source.shape, F32)
    strip_shape = pltpu.VMEM(padded(COUNT), F32)
    kept, corrected, final = pl.pallas_call(
        functools.partial(early_rows, plan, sizes),
        out_shape=(jax.ShapeDtypeStruct(padded(len(plan.kept)), F32), flat, flat),
        in_specs=[smem] + [vmem] * 6,
        out_specs=(vmem, vmem, vmem),
        scratch_shapes=[pltpu.VMEM(padded(len(plan.early)), F32), strip_shape],
        compiler_params=params(32),
        cost_estimate=pl.CostEstimate(flops=EARLY_FLOPS, bytes_accessed=0, transcendentals=0),
        name="early_rows",
    )(place, table, held, own, got_a, got_b, rows_a)
    corrected, final, _, _ = pl.pallas_call(
        functools.partial(late_rows, plan, sizes),
        out_shape=(flat,) * 4,
        in_specs=[smem] + [vmem] * 11,
        out_specs=(hbm, hbm, vmem, vmem),
        input_output_aliases={10: 2, 11: 3},
        scratch_shapes=[
            pltpu.VMEM(padded(len(plan.late)), F32),
            strip_shape,
            pltpu.SemaphoreType.DMA((2 * RUNS,)),
        ],
        compiler_params=params(32),
        name="late_rows",
    )(place, table, own, got_a, got_b, rows_a, corner_a, rows_b, corner_b, kept, corrected, final)
    return corrected.reshape(right_side.shape), final.reshape(right_side.shape)


def solution(mesh):
    return jax.shard_map(
        local,
        mesh=mesh,
        in_specs=(P(None, None, "gx", "gy"), P(None, "gx", "gy"), P()),
        out_specs=(P(None, None, "gx", "gy"), P(None, None, "gx", "gy")),
        check_vma=False,
    )
```

```python
import functools

import jax
import jax.numpy as jnp
from jax import lax
from jax.experimental import pallas as pl
from jax.experimental.pallas import tpu as pltpu
from jax.sharding import PartitionSpec as P

OMEGA_EDGE = 0.6
OMEGA_NODE = 0.7
F32 = jnp.float32
LANES = 128
TILE = 8
REACH = 2
WIDE = 2 * REACH
COLS = 2 * WIDE
EARLY_FLOPS = 10**10
RUNS = 4
PAD = 8


def lanes():
    return lax.broadcasted_iota(jnp.int32, (TILE, LANES), 1)


def class_table(conductivity):
    row = jnp.pad(conductivity, (1, LANES - 1 - conductivity.shape[0]))
    return jnp.broadcast_to(row[None], (TILE, LANES))


def pick(table, index):
    return jnp.take_along_axis(table, index, axis=1)


def turn(value, amount):
    amount = amount % LANES
    return value if amount == 0 else pltpu.roll(value, amount, 1)


def code(material):
    return (material + 1).astype(F32)


def gather(cells_x, place, fields, load, merge, edges, rows_a, rows_b, held):
    depth = edges.shape[0]
    lane = lanes()
    even = place[0] % 2 == 0
    row_a = jnp.where(even, cells_x - REACH, 0)
    row_b = jnp.where(even, 0, cells_x - REACH)
    for base in range(0, depth, TILE):
        where = pl.ds(base, TILE)
        packed = edges[where, :] if merge else jnp.zeros((TILE, LANES), F32)
        for field in fields:
            for row in range(cells_x):
                slot = (field * cells_x + row) * WIDE
                value = load(field, base, row)
                held[field, row, where, :] = value
                value = turn(value, slot + REACH)
                packed = jnp.where((lane >= slot) & (lane < slot + WIDE), value, packed)
            for out, first in ((rows_a, row_a), (rows_b, row_b)):
                for row in range(REACH):
                    out[row * 4 + field, where, :] = load(field, base, first + row)
        edges[where, :] = packed


def gather_classes(cells_x, place, material, edges, *outs):
    def load(field, base, row):
        return code(material[pl.ds(base * cells_x + row, TILE, stride=cells_x), :])

    gather(cells_x, place, (3,), load, False, edges, *outs)


def gather_source(cells_x, place, source, _edges, _rows_a, _rows_b, _held, edges, *outs):
    def load(field, base, row):
        return source[field, pl.ds(base * cells_x + row, TILE, stride=cells_x), :]

    gather(cells_x, place, range(3), load, True, edges, *outs)


def strip_index(cells_x, field, row, column):
    return (field * cells_x + row) * WIDE + column % WIDE


def strip_source(column, own, left, right):
    return jnp.where(column < REACH, left, jnp.where(column < COLS - REACH, own, right))


def corner_strips(cells_x, place, own, got_a, got_b, out):
    depth = own.shape[0]
    lane = lanes()
    per_field = LANES // 4
    field, rank, column = lane // per_field, (lane % per_field) // COLS, lane % COLS
    row = jnp.where(rank < REACH, rank, cells_x - 2 * REACH + rank)
    index = strip_index(cells_x, field, row, column)
    even = place[1] % 2 == 0
    for base in range(0, depth, TILE):
        where = pl.ds(base, TILE)
        mine, a, b = (pick(ref[where, :], index) for ref in (own, got_a, got_b))
        left, right = jnp.where(even, b, a), jnp.where(even, a, b)
        out[where, :] = strip_source(column, mine, left, right)


(SX, FX, FY, FZ, FACE_X, FACE_Y, FACE_Z, COEF, Q_Y) = range(9)
(RES_X, RES_Y, RES_Z, NODE, PHI, FLOW_Y, PSI_X, PSI_Y, PSI_Z) = range(9, 18)
(PHI2, MID_X, MID_Y, MID_Z, TURN_X, TURN_Y, TURN_Z, BACK_SX, OUT) = range(18, 27)
COUNT = OUT

READS = {
    SX: (),
    FX: (),
    FY: (),
    FZ: (),
    FACE_X: ((FY, 0), (FZ, 0)),
    FACE_Y: ((FZ, 0), (FZ, 1), (FX, 0)),
    FACE_Z: ((FX, 0), (FY, 0), (FY, 1)),
    BACK_SX: ((SX, 0),),
    COEF: ((SX, 0), (SX, -1), (BACK_SX, 0)),
    Q_Y: ((FY, 0), (SX, 0)),
    RES_X: ((FX, 0), (SX, 0), (FACE_Z, 0), (FACE_Y, 0)),
    RES_Y: ((Q_Y, 0), (FACE_Z, -1), (FACE_Z, 0), (FACE_X, 0)),
    RES_Z: ((FZ, 0), (SX, 0), (FACE_X, 0), (FACE_Y, 0), (FACE_Y, -1)),
    NODE: ((FX, 0), (SX, 0), (FX, -1), (SX, -1), (Q_Y, 0), (FZ, 0)),
    PHI: ((COEF, 0), (NODE, 0)),
    FLOW_Y: ((SX, 0), (PHI, 0)),
    PSI_X: ((RES_X, 0), (RES_X, -1), (SX, 0), (SX, -1)),
    PSI_Y: ((RES_Y, 0), (SX, 0), (BACK_SX, 0)),
    PSI_Z: ((RES_Z, 0), (SX, 0)),
    PHI2: (
        (SX, 0),
        (SX, -1),
        (PHI, 0),
        (PHI, 1),
        (PHI, -1),
        (FLOW_Y, 0),
        (COEF, 0),
        (NODE, 0),
    ),
    MID_X: ((PSI_X, 0), (PSI_X, 1)),
    MID_Y: ((PSI_Y, 0),),
    MID_Z: ((PSI_Z, 0),),
    TURN_X: ((MID_Y, 0), (MID_Z, 0)),
    TURN_Y: ((MID_Z, 0), (MID_Z, 1), (MID_X, 0)),
    TURN_Z: ((MID_X, 0), (MID_Y, 0), (MID_Y, 1)),
    OUT: (
        (TURN_X, 0),
        (TURN_Y, 0),
        (TURN_Y, -1),
        (TURN_Z, 0),
        (TURN_Z, -1),
        (PHI2, 0),
        (PHI2, 1),
        (MID_X, 0),
        (MID_Y, 0),
        (MID_Z, 0),
        (FX, 0),
        (FY, 0),
        (FZ, 0),
        (SX, 0),
        (RES_X, 0),
        (RES_Y, 0),
        (RES_Z, 0),
    ),
}
Z_READ = (SX, FX, FY, FZ, FACE_X, FACE_Y, RES_Z, PHI)
Z_READ += (PHI2, PSI_Z, MID_X, MID_Y, TURN_X, TURN_Y)
PASSES = (
    (SX, FX, FY, FZ),
    (FACE_X, FACE_Y, FACE_Z, BACK_SX, COEF, Q_Y),
    (RES_X, RES_Y, RES_Z, NODE, PHI),
    (FLOW_Y, PSI_X, PSI_Y, PSI_Z),
    (PHI2, MID_X, MID_Y, MID_Z),
    (TURN_X, TURN_Y, TURN_Z),
    (OUT,),
)


class Plan:
    def __init__(self, cells_x):
        self.cells_x = cells_x
        need = {(OUT, row) for row in range(cells_x)}
        todo = list(need)
        while todo:
            name, row = todo.pop()
            for read, offset in READS[name]:
                if (read, row + offset) not in need:
                    need.add((read, row + offset))
                    todo.append((read, row + offset))

        def early(name, row):
            if not READS[name]:
                return 0 <= row < cells_x
            return all(early(read, row + offset) for read, offset in READS[name])

        need = sorted(need)
        self.early = [item for item in need if early(*item)]
        self.late = [item for item in need if not early(*item)]
        used = {(read, row + offset) for name, row in self.late for read, offset in READS[name]}
        self.kept = [item for item in self.early if item in used]


def run_cycle(plan, late, sizes, place, table, fetch, strips, slots, strip_ref, emit, depth, leave=None):
    cells_x = plan.cells_x
    rows = cells_x + 2 * REACH
    lane = lanes()
    level = lax.broadcasted_iota(jnp.int32, (TILE, LANES), 0)
    has_low = jnp.where(place[0] > 0, 1.0, 0.0).astype(F32)
    has_high = jnp.where(place[0] < sizes[0] - 1, 1.0, 0.0).astype(F32)
    first_col = jnp.where(place[1] > 0, 4.0, 0.0).astype(F32)
    todo = plan.late if late else plan.early
    strip = None

    zeros = jnp.zeros((PAD, LANES), F32)
    for name, row in todo:
        if name in Z_READ:
            ref, slot = slots[name, row]
            ref[slot, pl.ds(0, PAD), :] = zeros
            ref[slot, pl.ds(PAD + depth, PAD), :] = zeros
    for name in Z_READ:
        strip_ref[name, pl.ds(0, PAD), :] = zeros
        strip_ref[name, pl.ds(PAD + depth, PAD), :] = zeros

    strip_row = lane // COLS - REACH
    column = lane % COLS
    strip_col = jnp.where(column < WIDE, column - REACH, column - WIDE - REACH + LANES)

    def inside(index, axis, length):
        at = index + place[axis] * length
        return (at >= 0) & (at < sizes[axis] * length)

    held = lane < rows * COLS
    if not late:
        held &= (strip_row >= 0) & (strip_row < cells_x)
    in_x, in_y = inside(strip_row, 0, cells_x), inside(strip_col, 1, LANES)
    strip_mask = jnp.where(in_x & in_y & held, 1.0, 0.0).astype(F32)
    strip_back_x = jnp.where(inside(strip_row - 1, 0, cells_x), 8.0, 4.0).astype(F32)
    strip_back_y = jnp.where(inside(strip_col - 1, 1, LANES), 8.0, 4.0).astype(F32)
    main_back_y = 4.0 + jnp.where(lane == 0, first_col, 4.0).astype(F32)

    def mask(row):
        if row is strip:
            return strip_mask
        if row < 0:
            return has_low
        return has_high if row >= cells_x else None

    def masked(value, row):
        m = mask(row)
        return value if m is None else value * m

    def over(top, bottom, row):
        m = mask(row)
        return top / bottom if m is None else (top * m) / (bottom + (1.0 - m))

    def scale(sigma):
        return sigma * (2.0 / 3.0) + 20.0 / 3.0

    class At:
        def __init__(self, base):
            self.base = base
            self.seen = {}

        def where(self, name, row, dz=0):
            ref, slot = (strip_ref, name) if row is strip else slots[name, row]
            return ref, slot, pl.ds(self.base + PAD + dz, TILE)

        def __call__(self, name, row, dz=0):
            key = (name, row, dz)
            if key not in self.seen:
                ref, slot, rows_z = self.where(name, row, dz)
                self.seen[key] = ref[slot, rows_z, :]
            return self.seen[key]

        def put(self, name, row, value):
            ref, slot, rows_z = self.where(name, row)
            ref[slot, rows_z, :] = value
            self.seen[name, row, 0] = value

        def fz(self, name, row):
            return self(name, row, 1)

        def bz(self, name, row):
            return self(name, row, -1)

        def fx(self, name, row):
            return turn(self(name, row), -COLS) if row is strip else self(name, row + 1)

        def bx(self, name, row):
            return turn(self(name, row), COLS) if row is strip else self(name, row - 1)

        def fy(self, name, row):
            moved = turn(self(name, row), -1)
            if row is strip:
                return moved
            start = (row + REACH) * COLS + COLS - REACH
            edge = turn(self(name, strip), LANES - 1 - start)
            return jnp.where(lane == LANES - 1, edge, moved)

        def by(self, name, row):
            moved = turn(self(name, row), 1)
            if row is strip:
                return moved
            edge = turn(self(name, strip), -((row + REACH) * COLS + REACH - 1))
            return jnp.where(lane == 0, edge, moved)

    def first_pass(at, row, names):
        x, y, z, codes = strips(at.base) if row is strip else fetch(at.base, row)
        sigma = pick(table, codes.astype(jnp.int32))
        weight = OMEGA_EDGE / (4.0 + sigma)
        for name, value in ((SX, sigma), (FX, x * weight), (FY, y * weight), (FZ, z * weight)):
            if name in names:
                at.put(name, row, value)

    def face_pass(at, row, names):
        if FACE_X in names:
            value = at(FY, row) - at.fz(FY, row) + at.fy(FZ, row) - at(FZ, row)
            at.put(FACE_X, row, masked(value, row))
        if FACE_Y in names:
            value = at(FZ, row) - at.fx(FZ, row) + at.fz(FX, row) - at(FX, row)
            at.put(FACE_Y, row, masked(value, row))
        if FACE_Z in names:
            value = at(FX, row) - at.fy(FX, row) + at.fx(FY, row) - at(FY, row)
            at.put(FACE_Z, row, masked(value, row))
        if BACK_SX in names:
            at.put(BACK_SX, row, at.by(SX, row))
        if COEF in names:
            diag = 3.0 * at(SX, row) + at.bx(SX, row) + at(BACK_SX, row) + at.bz(SX, row)
            at.put(COEF, row, over(OMEGA_NODE, diag, row))
        if Q_Y in names:
            at.put(Q_Y, row, at(FY, row) * scale(at(SX, row)))

    def residual_pass(at, row, names):
        g = scale(at(SX, row))
        if RES_X in names:
            z, y = at(FACE_Z, row), at(FACE_Y, row)
            edge = z - at.by(FACE_Z, row) - y + at.bz(FACE_Y, row)
            at.put(RES_X, row, at(FX, row) * g - edge)
        if RES_Y in names:
            z, x = at(FACE_Z, row), at(FACE_X, row)
            edge = at.bx(FACE_Z, row) - z + x - at.bz(FACE_X, row)
            at.put(RES_Y, row, at(Q_Y, row) - edge)
        if RES_Z in names:
            x, y = at(FACE_X, row), at(FACE_Y, row)
            edge = at.by(FACE_X, row) - x + y - at.bx(FACE_Y, row)
            at.put(RES_Z, row, at(FZ, row) * g - edge)
        if NODE in names:
            q_x = at(FX, row) * g
            if row is strip:
                back_x = turn(q_x, COLS)
            else:
                back_x = at(FX, row - 1) * scale(at(SX, row - 1))
            back_z = at.bz(FZ, row) * scale(at.bz(SX, row))
            change_y = at.by(Q_Y, row) - at(Q_Y, row)
            at.put(NODE, row, back_x - q_x + change_y + back_z - at(FZ, row) * g)
        if PHI in names:
            at.put(PHI, row, at(COEF, row) * at(NODE, row))

    def flow_pass(at, row, names):
        if FLOW_Y in names:
            at.put(FLOW_Y, row, at(SX, row) * (at.fy(PHI, row) - at(PHI, row)))
        if row is strip:
            const_x, const_y = strip_back_x, strip_back_y
        else:
            const_y = main_back_y
            const_x = 4.0 + 4.0 * has_low if row in (-1, 0) else 8.0
        const_z = jnp.where(level == 0, 4.0, 8.0).astype(F32) if at.base == 0 else 8.0
        for f, (const, back) in enumerate(((const_x, at.bx), (const_y, at.by), (const_z, at.bz))):
            if PSI_X + f in names:
                behind = at(BACK_SX, row) if f == 1 else back(SX, row)
                total = at(SX, row) + behind + const
                value = at(RES_X + f, row) + back(RES_X + f, row)
                at.put(PSI_X + f, row, over(value, total, row))

    def middle_pass(at, row, names):
        if PHI2 in names:
            sigma, phi = at(SX, row), at(PHI, row)
            flow_x = sigma * (at.fx(PHI, row) - phi)
            back_x = at.bx(SX, row) * (phi - at.bx(PHI, row))
            flow_z = sigma * (at.fz(PHI, row) - phi)
            back_z = at.bz(SX, row) * (phi - at.bz(PHI, row))
            change_y = at.by(FLOW_Y, row) - at(FLOW_Y, row)
            applied = back_x - flow_x + change_y + back_z - flow_z
            at.put(PHI2, row, phi + at(COEF, row) * (at(NODE, row) - applied))
        for f, ahead in enumerate((at.fx, at.fy, at.fz)):
            if MID_X + f in names:
                at.put(MID_X + f, row, 0.5 * (at(PSI_X + f, row) + ahead(PSI_X + f, row)))

    def turn_pass(at, row, names):
        if TURN_X in names:
            value = at(MID_Y, row) - at.fz(MID_Y, row) + at.fy(MID_Z, row) - at(MID_Z, row)
            at.put(TURN_X, row, masked(value, row))
        if TURN_Y in names:
            value = at(MID_Z, row) - at.fx(MID_Z, row) + at.fz(MID_X, row) - at(MID_X, row)
            at.put(TURN_Y, row, masked(value, row))
        if TURN_Z in names:
            value = at(MID_X, row) - at.fy(MID_X, row) + at.fx(MID_Y, row) - at(MID_Y, row)
            at.put(TURN_Z, row, masked(value, row))

    def last_pass(at, row, names):
        sigma, phi = at(SX, row), at(PHI2, row)
        x, y, z = at(TURN_X, row), at(TURN_Y, row), at(TURN_Z, row)
        edges = (
            z - at.by(TURN_Z, row) - y + at.bz(TURN_Y, row),
            at.bx(TURN_Z, row) - z + x - at.bz(TURN_X, row),
            at.by(TURN_X, row) - x + y - at.bx(TURN_Y, row),
        )
        for f, ahead in enumerate((at.fx, at.fy, at.fz)):
            change = ahead(PHI2, row) - phi + at(MID_X + f, row)
            final = at(RES_X + f, row) - edges[f] - sigma * change
            emit(at.base, row, f, at(FX + f, row) + change, final)

    steps = (first_pass, face_pass, residual_pass, flow_pass, middle_pass, turn_pass, last_pass)
    for names, step in zip(PASSES, steps):
        wanted = [item for item in todo if item[0] in names]
        rows_now = ([] if step is last_pass else [strip]) + sorted({row for _, row in wanted})
        for row in rows_now:
            here = names if row is strip else [name for name in names if (name, row) in wanted]
            for base in range(0, depth, TILE):
                if step is not last_pass:
                    step(At(base), row, here)
    for base in range(0, depth, TILE):
        for row in sorted(row for name, row in todo if name == OUT):
            last_pass(At(base), row, (OUT,))
        if leave is not None:
            leave(base)


def strip_reader(cells_x, place, own, got_a, got_b, corner_a, corner_b):
    lane = lanes()
    rows = cells_x + 2 * REACH
    row = jnp.clip(lane // COLS - REACH, 0, cells_x - 1)
    column = lane % COLS
    index = [strip_index(cells_x, f, row, column) for f in range(4)]
    even_x, even_y = place[0] % 2 == 0, place[1] % 2 == 0
    per_field = LANES // 4
    far = (rows - REACH) * COLS

    def strips(base):
        where = pl.ds(base, TILE)
        mine, a, b = own[where, :], got_a[where, :], got_b[where, :]
        left, right = jnp.where(even_y, b, a), jnp.where(even_y, a, b)
        if corner_a is not None:
            a, b = corner_a[where, :], corner_b[where, :]
            low, high = jnp.where(even_x, b, a), jnp.where(even_x, a, b)
        values = []
        for f in range(4):
            v = strip_source(column, pick(mine, index[f]), pick(left, index[f]), pick(right, index[f]))
            v = jnp.where((lane < REACH * COLS) | (lane >= far), 0.0, v)
            if corner_a is not None:
                moved = turn(low, -(f * per_field + REACH * COLS))
                v = jnp.where(lane < REACH * COLS, moved, v)
                moved = turn(high, far - f * per_field)
                v = jnp.where((lane >= far) & (lane < rows * COLS), moved, v)
            values.append(v)
        return values

    return strips


def writer(cells_x, corrected, final):
    def emit(base, row, f, value, rest):
        where = pl.ds(base * cells_x + row, TILE, stride=cells_x)
        corrected[f, where, :] = value
        final[f, where, :] = rest

    return emit


def early_rows(
    plan,
    sizes,
    place,
    table,
    held,
    own,
    got_a,
    got_b,
    rows_a,
    kept,
    corrected,
    final,
    scratch,
    strip_ref,
):
    cells_x = plan.cells_x

    def fetch(base, row):
        return [held[f, row, pl.ds(base, TILE), :] for f in range(4)]

    strips = strip_reader(cells_x, place, own, got_a, got_b, None, None)
    slots = {item: (kept, i) for i, item in enumerate(plan.kept)}
    others = [item for item in plan.early if item not in slots and item[0] != OUT]
    slots |= {item: (scratch, i) for i, item in enumerate(others)}
    table = table[...]
    emit = writer(cells_x, corrected, final)
    run_cycle(plan, False, sizes, place, table, fetch, strips, slots, strip_ref, emit, own.shape[0])


def late_rows(
    plan,
    sizes,
    place,
    table,
    own,
    got_a,
    got_b,
    rows_a,
    corner_a,
    rows_b,
    corner_b,
    kept,
    _part_corrected,
    _part_final,
    corrected,
    final,
    part_corrected,
    part_final,
    scratch,
    strip_ref,
    sems,
):
    cells_x = plan.cells_x
    even = place[0] % 2 == 0
    depth = own.shape[0]
    copies = []

    def leave(base):
        step = depth // RUNS
        if (base + TILE) % step == 0:
            where = pl.ds((base + TILE - step) * cells_x, step * cells_x)
            for source, target in ((part_corrected, corrected), (part_final, final)):
                copy = pltpu.make_async_copy(
                    source.at[:, where, :], target.at[:, where, :], sems.at[len(copies)]
                )
                copy.start()
                copies.append(copy)

    def fetch(base, row):
        first = (row + REACH if row < 0 else row - cells_x) * 4
        values = []
        for f in range(4):
            a, b = (ref[first + f, pl.ds(base, TILE), :] for ref in (rows_a, rows_b))
            values.append(jnp.where(even, b, a) if row < 0 else jnp.where(even, a, b))
        return values

    strips = strip_reader(cells_x, place, own, got_a, got_b, corner_a, corner_b)
    slots = {item: (kept, i) for i, item in enumerate(plan.kept)}
    others = [item for item in plan.late if item[0] != OUT]
    slots |= {item: (scratch, i) for i, item in enumerate(others)}
    table = table[...]
    emit = writer(cells_x, part_corrected, part_final)
    run_cycle(plan, True, sizes, place, table, fetch, strips, slots, strip_ref, emit, depth, leave)
    for copy in copies:
        copy.wait()


def swaps(count, first):
    pairs = [(i, i + 1) for i in range(first, count - 1, 2)]
    return pairs + [(j, i) for i, j in pairs]


def local(right_side, material, conductivity):
    depth, cells_x, cells_y = material.shape
    size_x, size_y = lax.axis_size("gx"), lax.axis_size("gy")
    place = jnp.stack([lax.axis_index("gx"), lax.axis_index("gy")]).astype(jnp.int32)
    table = class_table(conductivity)
    source = right_side.reshape(3, depth * cells_x, cells_y)
    classes = material.reshape(depth * cells_x, cells_y)
    vmem = pl.BlockSpec(memory_space=pltpu.VMEM)
    hbm = pl.BlockSpec(memory_space=pltpu.HBM)
    smem = pl.BlockSpec(memory_space=pltpu.SMEM)
    slab = jax.ShapeDtypeStruct((depth, cells_y), F32)

    def slabs(count):
        return jax.ShapeDtypeStruct((count, depth, cells_y), F32)

    def padded(count):
        return (count, depth + 2 * PAD, cells_y)

    def params(mib):
        return pltpu.CompilerParams(vmem_limit_bytes=mib * 2**20)

    outs = (
        slab,
        slabs(4 * REACH),
        slabs(4 * REACH),
        jax.ShapeDtypeStruct((4, cells_x, depth, cells_y), F32),
    )
    outs = pl.pallas_call(
        functools.partial(gather_classes, cells_x),
        out_shape=outs,
        in_specs=[smem, vmem],
        out_specs=(vmem,) * 4,
        compiler_params=params(16),
        cost_estimate=pl.CostEstimate(flops=10**9, bytes_accessed=1000, transcendentals=0),
        name="gather_classes",
    )(place, classes)
    own, rows_a, rows_b, held = pl.pallas_call(
        functools.partial(gather_source, cells_x),
        out_shape=tuple(jax.ShapeDtypeStruct(out.shape, F32) for out in outs),
        in_specs=[smem] + [vmem] * 5,
        out_specs=(vmem,) * 4,
        input_output_aliases={2: 0, 3: 1, 4: 2, 5: 3},
        compiler_params=params(16),
        name="gather_source",
    )(place, source, *outs)
    got_b = lax.ppermute(own, "gy", swaps(size_y, 1))
    got_a = lax.ppermute(own, "gy", swaps(size_y, 0))
    corners = pl.pallas_call(
        functools.partial(corner_strips, cells_x),
        out_shape=slab,
        in_specs=[smem] + [vmem] * 3,
        out_specs=vmem,
        compiler_params=params(16),
        name="corner_strips",
    )(place, own, got_a, got_b)
    corner_a = lax.ppermute(corners, "gx", swaps(size_x, 0))
    corner_b = lax.ppermute(corners, "gx", swaps(size_x, 1))
    rows_b = lax.ppermute(rows_b, "gx", swaps(size_x, 1))
    rows_a = lax.ppermute(rows_a, "gx", swaps(size_x, 0))

    plan, sizes = Plan(cells_x), (size_x, size_y)
    flat = jax.ShapeDtypeStruct(source.shape, F32)
    strip_shape = pltpu.VMEM(padded(COUNT), F32)
    kept, corrected, final = pl.pallas_call(
        functools.partial(early_rows, plan, sizes),
        out_shape=(jax.ShapeDtypeStruct(padded(len(plan.kept)), F32), flat, flat),
        in_specs=[smem] + [vmem] * 6,
        out_specs=(vmem, vmem, vmem),
        scratch_shapes=[pltpu.VMEM(padded(len(plan.early)), F32), strip_shape],
        compiler_params=params(32),
        cost_estimate=pl.CostEstimate(flops=EARLY_FLOPS, bytes_accessed=0, transcendentals=0),
        name="early_rows",
    )(place, table, held, own, got_a, got_b, rows_a)
    corrected, final, _, _ = pl.pallas_call(
        functools.partial(late_rows, plan, sizes),
        out_shape=(flat,) * 4,
        in_specs=[smem] + [vmem] * 11,
        out_specs=(hbm, hbm, vmem, vmem),
        input_output_aliases={10: 2, 11: 3},
        scratch_shapes=[
            pltpu.VMEM(padded(len(plan.late)), F32),
            strip_shape,
            pltpu.SemaphoreType.DMA((2 * RUNS,)),
        ],
        compiler_params=params(32),
        name="late_rows",
    )(place, table, own, got_a, got_b, rows_a, corner_a, rows_b, corner_b, kept, corrected, final)
    return corrected.reshape(right_side.shape), final.reshape(right_side.shape)


def solution(mesh):
    return jax.shard_map(
        local,
        mesh=mesh,
        in_specs=(P(None, None, "gx", "gy"), P(None, "gx", "gy"), P()),
        out_specs=(P(None, None, "gx", "gy"), P(None, None, "gx", "gy")),
        check_vma=False,
    )
```
